32 devices in a mesh: member: 1, tile: 32 (over z, y, x, core).
Axes of the slice: x: 2, y: 2, z: 4, core: 2. Of those that a mesh axis runs over, the one named last changes fastest.
Arguments:
- forcing: bfloat16 [128, 8, 10, 128], P(('member', 'tile')), may hold values from -6 to 6
- ice_state: bfloat16 [1024, 128, 128], P(('member', 'tile')), may hold values from -6 to 6
- sensitivity: bfloat16 [1024, 128, 128], P(('member', 'tile')), may hold values from -6 to 6
- owner_device: int32 [1024, 4], P('tile'), may hold values from 0 to 31, all different within a row; in each aligned block of 32 rows (0 to 31, 32 to 63, ...) at most 8 rows name the same one
- panel_slot: int32 [1024, 4], P('tile'), may hold values from 0 to 3
- row_offset: int32 [1024, 4], P('tile'), may hold values from 0 to 7
- intersection_weight: float32 [1024, 4], P('tile'), may hold values from 0.2 to 1
- col_map: float32 [128, 128], replicated, may hold values from 0 to 1
- ocean_mask: int32 [1024, 128], P('tile'), may hold values 0 or 1
- lift_weight: bfloat16 [10, 128], replicated, may hold values from -1 to 1
- conv_weight: bfloat16 [3, 3, 3, 128, 128], replicated, may hold values from -0.1875 to 0.1875
- conv_bias: float32 [3, 128], replicated, may hold values from -3 to 3
Outputs:
- imitated: bfloat16 [1024, 128, 128], P(('member', 'tile'))
- state_grad: bfloat16 [1024, 128, 128], P(('member', 'tile'))
- forcing_grad: float32 [128, 8, 10, 128], P(('member', 'tile'))
The draws below stay inside these ranges and needn't reach their ends.
Inputs may be any that keep to these rules, and one draw needn't show every extreme that they name: `owner_device`: each ice row names 4 different owners; in the rows of one device no owner is named by more than 8 intersections, and that count is reached.
All inputs are finite; a program needn't handle non-finite values. No bound on the sum of `ocean_mask` on one device may be relied on, other than what follows from the above.
Results may differ from the reference program's by a relative error of at most 0.015.
Values may be sent and summed in bfloat16 or wider, within the bound.
No kernel may reach another device: no remote copies, remote signals or barrier semaphores. Data moves between devices by JAX's collectives and lax.ppermute only.
A program may use at most 128 MiB of HBM per device.

```python
import math
import jax
import jax.numpy as jnp
import numpy as np
from jax import lax

C = 128
F = 10
L = 3
K = 4
PC = 128
COLS = 128
ROWS_DEV = 32
PR = 8
PAN_DEV = 4
ROWS = 1024
NPAN = 128
OWNERS = 32
CAP = 8


def draw_col_map(key, part):
    row_pos = jnp.arange(PC, dtype=jnp.int32)[:, None]
    col_pos = jnp.arange(COLS, dtype=jnp.int32)[None, :]
    centre = col_pos * PC // COLS
    inside = jnp.abs(row_pos - centre) <= 1
    values = jax.random.uniform(key, (PC, COLS), jnp.float32, 0.2, 1.0)
    return jnp.where(inside, values, jnp.float32(0.0)).astype(jnp.float32)


def place_ends(result, stream_key, smallest, high):
    shape = result.shape
    place = [jax.random.randint(jax.random.fold_in(stream_key, axis), (), 0, shape[axis]) for axis in range(len(shape))]
    result = result.at[tuple(place)].set(smallest)
    longest = shape.index(max(shape))
    place[longest] = (place[longest] + 1) % shape[longest]
    return result.at[tuple(place)].set(high)


def shard_levels(own_key, dims, pieces, low, top_value):
    level, own = 1.0, jax.random.fold_in(own_key, 6)
    for dim, shards_of in pieces:
        steps = jnp.exp(jax.random.uniform(jax.random.fold_in(own, dim), (shards_of,), jnp.float32, low / len(pieces), top_value / len(pieces)))
        level = level * jnp.repeat(steps, dims[dim] // shards_of).reshape([-1 if axis == dim else 1 for axis in range(len(dims))])
    return level


def assign_block(stream_key, own, number, rows, count, top, limit, slope):
    order = jax.random.permutation(stream_key, count)
    heavy_load, common = load_shares(count, rows * top, limit, slope, True), load_shares(count, rows * top, limit, slope, False)
    places = jnp.arange(count)

    def named(sizes, offset_by):
        used = int((sizes > 0).sum())
        fixed = max(1, used // 4)
        passed = fixed + (places - fixed + offset_by * (used - fixed)) % max(1, count - fixed)
        return jnp.zeros((count,), jnp.int32).at[order[jnp.where(places < fixed, places, passed)]].set(jnp.asarray(sizes, jnp.int32))

    sizes = jnp.where(number % 4 == 0, named(heavy_load, number // 4), named(common, number - number // 4 - 1))
    mixed = jax.random.permutation(jax.random.fold_in(own, 3), count)
    giver, taker = mixed[0:count // 2 * 2:2], mixed[1:count // 2 * 2:2]
    margin = jnp.minimum(sizes[giver] - 1, limit - sizes[taker]) // 2
    margin = jnp.where((giver == order[0]) | (taker == order[0]) | (sizes[taker] == 0), 0, jnp.maximum(margin, 0))
    passed = jax.random.randint(jax.random.fold_in(own, 4), (count // 2,), 0, 1 << 20) % (margin + 1)
    sizes = sizes.at[giver].add(-passed).at[taker].add(passed)
    items = jnp.searchsorted(jnp.cumsum(sizes), jnp.arange(rows * top), side="right").astype(jnp.int32)
    grid = items.reshape(top, rows).T
    grid = grid[jax.random.permutation(jax.random.fold_in(own, 1), rows)]
    offset_by = jax.random.randint(jax.random.fold_in(own, 2), (rows, 1), 0, top)
    return jnp.take_along_axis(grid, (jnp.arange(top)[None, :] + offset_by) % top, axis=1)


def load_shares(count, total, reach, lean, full):
    portions = [(1 << 20) // math.isqrt(rank ** lean) + 1 for rank in range(1, count + 1)]
    largest = reach if full else min(reach, max(-(-total // count), total * portions[0] // sum(portions)))
    least = 1 if total - largest >= count - 1 else 0
    given, surplus = [largest] + [least] * (count - 1), total - largest - least * (count - 1)
    while surplus > 0:
        free = [i for i in range(1, count) if given[i] < largest] or [i for i in range(1, count) if given[i] < reach]
        mass, left = sum([portions[i] for i in free]), surplus
        for i in free:
            addition = min(reach - given[i], max(1, left * portions[i] // mass), surplus)
            given[i] = given[i] + addition
            surplus = surplus - addition
    return np.array(given)


def scatter_about(own_key, shape, deviation, limit, cuts=(), kind=jnp.bfloat16):
    array = jax.random.normal(own_key, shape, jnp.float32) * deviation
    if len(cuts) > 0:
        array = shard_levels(own_key, shape, cuts, -0.22, 0.18) * array
    return jnp.clip(array, min=-limit, max=limit).astype(kind)


def setup_inputs(seed: int = 0, part: int = 0) -> dict:
    key_of = jax.random.split(jax.random.key(seed), 13)
    own_keys = jax.random.split(jax.random.fold_in(key_of[12], part), 13)
    forcing = scatter_about(own_keys[0], (NPAN, PR, F, PC), 1.0, 6.0, ((0, 32),))
    ice_state = scatter_about(own_keys[1], (ROWS, COLS, C), 1.0, 6.0, ((0, 32),))
    sensitivity = scatter_about(own_keys[2], (ROWS, COLS, C), 1.0, 6.0, ((0, 32),))
    owner_device_keys = jax.random.split(jax.random.fold_in(key_of[3], 1), ROWS // ROWS_DEV)
    owner_device_turns = jax.random.permutation(jax.random.fold_in(key_of[3], 3), ROWS // ROWS_DEV)
    owner_device = jax.vmap(lambda own, number: assign_block(jax.random.fold_in(key_of[3], 2), own, number, ROWS_DEV, OWNERS, K, CAP, 2))(owner_device_keys, owner_device_turns).reshape((ROWS, K))
    panel_slot = place_ends(jax.random.randint(key_of[4], (ROWS, K), 0, PAN_DEV), jax.random.fold_in(key_of[4], 1), 0, PAN_DEV - 1).astype(jnp.int32)
    row_offset = place_ends(jax.random.randint(key_of[5], (ROWS, K), 0, PR), jax.random.fold_in(key_of[5], 1), 0, PR - 1).astype(jnp.int32)
    intersection_weight = jnp.clip(jnp.exp(math.log(1.0) - 1.609438 * jax.random.uniform(key_of[6], (ROWS, K), jnp.float32) ** shard_levels(key_of[6], (ROWS, K), ((0, 32),), -0.2, 0.2)), 0.2, 1.0)
    col_map = draw_col_map(jax.random.fold_in(key_of[12], 71), part)
    ocean_mask = place_ends((jax.random.randint(key_of[8], (ROWS, COLS), 0, 4) < 3).astype(jnp.int32), jax.random.fold_in(key_of[8], 1), 0, 1)
    lift_weight = scatter_about(key_of[9], (F, C), (4 * F) ** -0.5, 1.0)
    conv_weight = scatter_about(key_of[10], (L, 3, 3, C, C), (9 * C) ** -0.5, 0.1875)
    conv_bias = scatter_about(key_of[11], (L, C), 0.5, 3.0, (), jnp.float32)
    return {"forcing": forcing, "ice_state": ice_state, "sensitivity": sensitivity, "owner_device": owner_device, "panel_slot": panel_slot, "row_offset": row_offset, "intersection_weight": intersection_weight, "col_map": col_map, "ocean_mask": ocean_mask, "lift_weight": lift_weight, "conv_weight": conv_weight, "conv_bias": conv_bias}


def convolve(field, kernel):
    return lax.conv_general_dilated(field[None].astype(jnp.float32), kernel.astype(jnp.float32), (1, 1), ((1, 1), (1, 1)), dimension_numbers=("NHWC", "HWIO", "NHWC"), precision=lax.Precision.HIGHEST)[0]


def reference(forcing, ice_state, sensitivity, owner_device, panel_slot, row_offset, intersection_weight, col_map, ocean_mask, lift_weight, conv_weight, conv_bias):
    highest = lax.Precision.HIGHEST
    flat_panels = forcing.reshape(NPAN * PR, F, PC)
    global_row = ((owner_device * PAN_DEV + panel_slot) * PR + row_offset).astype(jnp.int32)
    picked = flat_panels[global_row].astype(jnp.float32)
    mapped = jnp.einsum("rkfp,pc->rkfc", picked, col_map, precision=highest)
    ice_forcing = jnp.sum(intersection_weight[:, :, None, None] * mapped, axis=1).astype(jnp.bfloat16)
    lifted = jnp.einsum("rfc,fh->rch", ice_forcing.astype(jnp.float32), lift_weight.astype(jnp.float32), precision=highest)
    ocean_cells = ocean_mask.astype(jnp.float32)[:, :, None]
    hidden = ice_state
    tangents = []
    for layer_index in range(L):
        if layer_index == 1:
            hidden = (hidden.astype(jnp.float32) + lifted).astype(jnp.bfloat16)
        tangent = jnp.tanh(convolve(hidden, conv_weight[layer_index]) + conv_bias[layer_index])
        tangents.append(tangent)
        hidden = (hidden.astype(jnp.float32) + ocean_cells * tangent).astype(jnp.bfloat16)
    imitated = hidden
    adjoint = sensitivity.astype(jnp.float32)
    force_grad = jnp.zeros((ROWS, F, COLS), jnp.float32)
    for layer_index in reversed(range(L)):
        tangent = tangents[layer_index]
        delta_act = (adjoint * ocean_cells * (1.0 - tangent * tangent)).astype(jnp.bfloat16)
        flipped = jnp.flip(conv_weight[layer_index], (0, 1)).transpose(0, 1, 3, 2)
        adjoint = adjoint + convolve(delta_act, flipped)
        if layer_index == 1:
            force_grad = jnp.einsum("rch,fh->rfc", adjoint, lift_weight.astype(jnp.float32), precision=highest)
    projected = jnp.einsum("rfc,pc->rfp", force_grad, col_map, precision=highest)
    row_terms = intersection_weight[:, :, None, None] * projected[:, None]
    forcing_grad = jnp.zeros((NPAN * PR, F, PC), jnp.float32).at[global_row.reshape(-1)].add(row_terms.reshape(ROWS * K, F, PC))
    return imitated, adjoint.astype(jnp.bfloat16), forcing_grad.reshape(NPAN, PR, F, PC)
```

```python
import functools

import jax
import jax.numpy as jnp
from jax import lax
from jax.experimental import pallas as pl
from jax.experimental.pallas import tpu as pltpu
from jax.sharding import PartitionSpec as P

F = 10
FP = 16
K = 4
C = 128
ROWS = 32
EXT = 48
PAD = 8
GROUP = 8
PAIR = 2 * C
TAPS = 3 * C
BF = jnp.bfloat16
F32 = jnp.float32
MIB = 1 << 20


def params(mib):
    return pltpu.CompilerParams(vmem_limit_bytes=mib * MIB)


def dot(a, b, dims=(((1,), (0,)), ((), ()))):
    return lax.dot_general(a, b, dims, preferred_element_type=F32)


def split(x):
    high = x.astype(BF)
    return high, (x - high.astype(F32)).astype(BF)


def fine_dot(a, b, dims=(((1,), (0,)), ((), ()))):
    ah, al = split(a)
    bh, bl = split(b)
    return dot(ah, bh, dims) + (dot(ah, bl, dims) + dot(al, bh, dims))


def pair_rows(index, count=1):
    start = index * C
    if not isinstance(index, int):
        start = pl.multiple_of(start, C)
    return pl.ds(start, count * C)


def store_pair(xp, index, value):
    column = lax.broadcasted_iota(jnp.int32, (C, PAIR), 0)
    before = jnp.where(column == 0, 0.0, pltpu.roll(value, 1, 0)).astype(BF)
    after = jnp.where(column == C - 1, 0.0, pltpu.roll(value, C - 1, 0)).astype(BF)
    value = value.astype(BF)
    rows = pair_rows(index)
    for half in range(2):
        lanes = slice(half * C, half * C + C)
        for tap, part in enumerate((before, value, after)):
            start = half * TAPS + tap * C
            xp[rows, start : start + C] = part[:, lanes]


def centre(xp, index):
    low = xp[pair_rows(index), TAPS + C : TAPS + 2 * C]
    high = xp[pair_rows(index + 1), C : 2 * C]
    return jnp.concatenate([low, high], axis=1).astype(F32)


def two_rows(ref, row):
    start = row * C
    if not isinstance(row, int):
        start = pl.multiple_of(start, C)
    low = ref[pl.ds(start, C), :]
    high = ref[pl.ds(start + C, C), :]
    return jnp.concatenate([low, high], axis=1).astype(F32)


def layer(xp, weight, count, step, finish):
    def chunk(first, size):
        total = dot(xp[pair_rows(first, size), :], weight[: 2 * TAPS, :])
        total += dot(xp[pair_rows(first + 1, size), :], weight[2 * TAPS :, :])
        for j in range(size):
            finish(first + j, total[j * C : (j + 1) * C])

    full = count // step

    def body(i, carry):
        chunk(i * step, step)
        return carry

    lax.fori_loop(0, full, body, 0)
    if count % step:
        chunk(full * step, count % step)


def prep_kernel(forcing, owner, slot, offset, weight, fields, table):
    rows = forcing[...].reshape(ROWS, F, C).astype(F32)
    for f in range(F):
        fields[f * ROWS : (f + 1) * ROWS, :] = rows[:, f, :].astype(BF)
    ident = ((owner[...] * 4 + slot[...]) * 8 + offset[...]).astype(F32)
    lane = lax.broadcasted_iota(jnp.int32, (ROWS, C), 1)
    row = lax.broadcasted_iota(jnp.int32, (ROWS, C), 0)

    def spread(value):
        total = jnp.zeros((1, C), F32)
        for k in range(K):
            here = jnp.where(lane == k * ROWS + row, value[:, k : k + 1], 0.0)
            total += jnp.sum(here, axis=0, keepdims=True)
        return total

    block = jnp.concatenate(
        [spread(ident), spread(weight[...]), jnp.zeros((6, C), F32)], axis=0
    )
    table[...] = jnp.broadcast_to(block[None], table.shape)


def message_kernel(planes, table, *refs):
    blocks, outs, scatter, wide = refs[:planes], refs[planes:-2], refs[-2], refs[-1]
    me = lax.axis_index("tile")
    plane, spot = me // GROUP, me % GROUP
    count = planes * GROUP
    for z in range(planes):
        for f in range(F):
            wide[z * ROWS : (z + 1) * ROWS, f * C : (f + 1) * C] = blocks[z][
                f * ROWS : (f + 1) * ROWS, :
            ]
    sources = planes * ROWS
    lane = lax.broadcasted_iota(jnp.int32, (1, sources), 1)
    from_plane = lax.rem(plane - lane // ROWS + planes, planes)
    ident = ((from_plane * GROUP + spot) * ROWS + lane % ROWS).astype(F32)
    idents, weights = [], []
    for s in range(GROUP):
        mate = plane * GROUP + (spot ^ s)
        for step in (-1, 0, 1):
            device = mate + step
            inside = jnp.logical_and(device >= 0, device < count)
            entry = table[jnp.clip(device, 0, count - 1)]
            idents.append(entry[0:1])
            weights.append(jnp.where(inside, entry[1:2], 0.0))
    fill = [jnp.zeros((C - 3 * GROUP, C), F32)]
    idents = jnp.concatenate(idents + fill, axis=0).T
    weights = jnp.concatenate(weights + fill, axis=0).T
    picks = []
    for s in range(GROUP):
        parts = []
        for step, start, size in ((0, ROWS - PAD, PAD), (1, 0, ROWS), (2, 0, PAD)):
            col = 3 * s + step
            total = jnp.zeros((size, sources), F32)
            for k in range(K):
                rows = slice(k * ROWS + start, k * ROWS + start + size)
                named = idents[rows, col : col + 1] == ident
                total += jnp.where(named, weights[rows, col : col + 1], 0.0)
            parts.append(total)
        picks.append(jnp.concatenate(parts, axis=0))
    every = jnp.concatenate(picks, axis=0).astype(BF)
    for f in range(F):
        found = dot(every, wide[:, f * C : (f + 1) * C]).astype(BF)
        for s in range(GROUP):
            outs[s][f * EXT : (f + 1) * EXT, :] = found[s * EXT : (s + 1) * EXT]
    own = jnp.concatenate([pick[PAD : PAD + ROWS] for pick in picks], axis=0)
    scatter[...] = own.T.astype(BF)


def weight_kernel(weight, *outs):
    zero = jnp.zeros((TAPS, C), BF)
    for l in range(3):
        for back in range(2):
            out = outs[2 * l + back]
            out[0:TAPS, C:] = zero
            out[3 * TAPS :, :C] = zero
            for a in range(3):
                for b in range(3):
                    if back:
                        block = weight[l, 2 - a, 2 - b].astype(F32).T.astype(BF)
                    else:
                        block = weight[l, a, b]
                    for half in range(2):
                        start = (a + half) * TAPS + b * C
                        out[start : start + C, half * C : half * C + C] = block


def first_kernel(ice, low, high, mask, weight, bias, hidden, slope, ocean, xp):
    def ice_row(r):
        if r < 0:
            return low[(r + 6) * C : (r + 7) * C, :]
        if r >= ROWS:
            return high[(r - ROWS) * C : (r - ROWS + 1) * C, :]
        return ice[r]

    for p in range(22):
        row = 2 * p - 6
        store_pair(xp, p, jnp.concatenate([ice_row(row), ice_row(row + 1)], axis=1).astype(F32))
    edge = 9 * C
    cells = jnp.concatenate(
        [low[edge : edge + 8, :].astype(F32), mask[...].astype(F32), high[edge : edge + 8, :].astype(F32)],
        axis=0,
    )
    cells = jnp.concatenate([cells, jnp.zeros((C - EXT, C), F32)], axis=0).T
    for r in range(-5, 37):
        column = jnp.broadcast_to(cells[:, r + PAD : r + PAD + 1], (C, C))
        ocean[(r + 5) * C : (r + 6) * C, :] = column.astype(BF)
    both = jnp.concatenate([bias[0:1, :], bias[0:1, :]], axis=1)

    def finish(p, total):
        tangent = jnp.tanh(total + both)
        cell = two_rows(ocean, 2 * p)
        slope[pair_rows(p), :] = (cell * (1.0 - tangent * tangent)).astype(BF)
        hidden[pair_rows(p), :] = (centre(xp, p) + cell * tangent).astype(BF)

    layer(xp, weight, 21, 7, finish)


def main_kernel(*refs):
    messages = refs[:GROUP]
    (col_map, lift, bias, hidden, slope0, ocean, sens, low, high, w1f, w2f, w2b, w1b) = refs[
        GROUP : GROUP + 13
    ]
    imitated, act0, grad1, project = refs[GROUP + 13 : GROUP + 17]
    ice, lifted, diag, xa, xb, slope1, slope2, grads, out_rows, turned = refs[GROUP + 17 :]
    ice[...] = jnp.zeros(ice.shape, F32)
    for f in range(F):
        rows = slice(f * EXT, (f + 1) * EXT)
        total = messages[0][rows, :].astype(F32)
        for s in range(1, GROUP):
            total += messages[s][rows, :].astype(F32)
        ice[:, f, :] = fine_dot(total, col_map[...])
    diag[...] = jnp.zeros(diag.shape, BF)
    for j in range(GROUP):
        diag[j * FP : j * FP + F, j * C : (j + 1) * C] = lift[...]
    for group in range(EXT // GROUP):
        block = ice[group * GROUP : (group + 1) * GROUP].reshape(C, C)
        turned[group * C : (group + 1) * C, :] = block.T.astype(BF)
    for group in range(EXT // GROUP):
        lifted[group * C : (group + 1) * C, :] = dot(
            turned[group * C : (group + 1) * C, :], diag[...]
        )

    def lifted_row(r):
        e = r + PAD
        return lifted[(e // 8) * C : (e // 8 + 1) * C, (e % 8) * C : (e % 8 + 1) * C]

    for p in range(21):
        row = 2 * p - 5
        add = jnp.concatenate([lifted_row(row), lifted_row(row + 1)], axis=1)
        value = (hidden[pair_rows(p), :].astype(F32) + add).astype(BF)
        store_pair(xa, p, value.astype(F32))

    def bias_of(l):
        return jnp.concatenate([bias[l : l + 1, :], bias[l : l + 1, :]], axis=1)

    bias1, bias2 = bias_of(1), bias_of(2)

    def finish1(p, total):
        tangent = jnp.tanh(total + bias1)
        cell = two_rows(ocean, 2 * p + 1)
        slope1[pair_rows(p), :] = (cell * (1.0 - tangent * tangent)).astype(BF)
        value = (centre(xa, p) + cell * tangent).astype(BF)
        store_pair(xb, p, value.astype(F32))

    layer(xa, w1f, 20, 5, finish1)

    def finish2(p, total):
        tangent = jnp.tanh(total + bias2)
        cell = two_rows(ocean, 2 * p + 2)
        slope2[pair_rows(p), :] = (cell * (1.0 - tangent * tangent)).astype(BF)
        value = (centre(xb, p) + cell * tangent).astype(BF)
        out_rows[pair_rows(2 * p), :] = value[:, :C]
        out_rows[pair_rows(2 * p + 1), :] = value[:, C:]

    layer(xb, w2f, 19, 5, finish2)
    imitated[...] = out_rows[3 * C : 35 * C, :].reshape(ROWS, C, C)

    def sens_row(r):
        if r < 0:
            return low[(r + 9) * C : (r + 10) * C, :]
        if r >= ROWS:
            return high[(r - ROWS + 6) * C : (r - ROWS + 7) * C, :]
        return sens[r]

    for p in range(19):
        row = 2 * p - 3
        value = jnp.concatenate([sens_row(row), sens_row(row + 1)], axis=1).astype(F32)
        store_pair(xa, p, value * slope2[pair_rows(p), :].astype(F32))
        out_rows[pair_rows(2 * p), :] = sens_row(row)
        out_rows[pair_rows(2 * p + 1), :] = sens_row(row + 1)

    def finish3(p, total):
        total += two_rows(out_rows, 2 * p + 1)
        grads[pair_rows(2 * p), :] = total[:, :C]
        grads[pair_rows(2 * p + 1), :] = total[:, C:]
        store_pair(xb, p, total * slope1[pair_rows(p + 1), :].astype(F32))

    layer(xa, w2b, 18, 6, finish3)

    def finish4(p, total):
        total += two_rows(grads, 2 * p + 1)
        act0[pair_rows(p), :] = (total * slope0[pair_rows(p + 2), :].astype(F32)).astype(BF)
        grad1[pair_rows(2 * p), :] = total[:, :C]
        grad1[pair_rows(2 * p + 1), :] = total[:, C:]

    layer(xb, w1b, 17, 6, finish4)
    short = jnp.concatenate([lift[...].astype(F32), jnp.zeros((FP - F, C), F32)], axis=0).astype(BF)
    nt = (((1,), (1,)), ((), ()))
    for r in range(ROWS):
        part = dot(short, grad1[(r + 1) * C : (r + 2) * C, :].astype(BF), nt)
        ice[r, :, :] = part
    ice[0:ROWS] = fine_dot(ice[0:ROWS].reshape(ROWS * FP, C), col_map[...], nt).reshape(ROWS, FP, C)
    for f in range(F):
        project[f * ROWS : (f + 1) * ROWS, :] = ice[0:ROWS, f, :].astype(BF)


def last_kernel(act0, grad1, weight, out, xp):
    for p in range(17):
        store_pair(xp, p, act0[pair_rows(p), :].astype(F32))

    def finish(p, total):
        total += two_rows(grad1, 2 * p + 1)
        out[2 * p] = total[:, :C].astype(BF)
        out[2 * p + 1] = total[:, C:].astype(BF)

    layer(xp, weight, 16, 4, finish)


def scatter_kernel(planes, scatter, *refs):
    blocks, outs, wide = refs[:GROUP], refs[GROUP:-1], refs[-1]
    for s in range(GROUP):
        for f in range(F):
            wide[s * ROWS : (s + 1) * ROWS, f * C : (f + 1) * C] = blocks[s][
                f * ROWS : (f + 1) * ROWS, :
            ]
    for f in range(F):
        found = dot(scatter[...], wide[:, f * C : (f + 1) * C]).astype(BF)
        for z in range(planes):
            outs[z][f * ROWS : (f + 1) * ROWS, :] = found[z * ROWS : (z + 1) * ROWS]


def sum_kernel(planes, *refs):
    blocks, out = refs[:planes], refs[planes]
    for f in range(F):
        rows = slice(f * ROWS, (f + 1) * ROWS)
        total = blocks[0][rows, :].astype(F32)
        for z in range(1, planes):
            total += blocks[z][rows, :].astype(F32)
        out[:, f, :] = total


def shape(*dims, dtype=BF):
    return jax.ShapeDtypeStruct(dims, dtype)


def body(
    forcing,
    ice_state,
    sensitivity,
    owner_device,
    panel_slot,
    row_offset,
    intersection_weight,
    col_map,
    ocean_mask,
    lift_weight,
    conv_weight,
    conv_bias,
):
    count = lax.axis_size("tile")
    planes = count // GROUP

    def by_plane(step):
        return [(i, (i + GROUP * step) % count) for i in range(count)]

    def by_mate(step):
        return [(i, i ^ step) for i in range(count)]

    fields, table = pl.pallas_call(
        prep_kernel,
        out_shape=(shape(F * ROWS, C), shape(count, 8, C, dtype=F32)),
        name="prep",
    )(forcing, owner_device, panel_slot, row_offset, intersection_weight)
    blocks = [fields] + [lax.ppermute(fields, "tile", by_plane(z)) for z in range(1, planes)]
    table = lax.all_to_all(table, "tile", 0, 0, tiled=True)

    mask = ocean_mask.astype(BF)
    flat_ice = ice_state.reshape(ROWS * C, C)
    flat_sens = sensitivity.reshape(ROWS * C, C)
    to_next = jnp.concatenate([flat_ice[26 * C :], flat_sens[29 * C :], mask[24:], mask[24:]], axis=0)
    to_last = jnp.concatenate([flat_ice[: 6 * C], flat_sens[: 3 * C], mask[:8], mask[:8]], axis=0)
    forward = [(i, i + 1) for i in range(count - 1)]
    low = lax.ppermute(to_next, "tile", forward)
    high = lax.ppermute(to_last, "tile", [(b, a) for a, b in forward])

    weights = pl.pallas_call(
        weight_kernel,
        out_shape=tuple(shape(4 * TAPS, PAIR) for _ in range(6)),
        compiler_params=params(32),
        name="taps",
        cost_estimate=pl.CostEstimate(flops=0, bytes_accessed=6 * MIB, transcendentals=0),
    )(conv_weight)

    *messages, scatter = pl.pallas_call(
        functools.partial(message_kernel, planes),
        out_shape=tuple(shape(F * EXT, C) for _ in range(GROUP)) + (shape(planes * ROWS, GROUP * ROWS),),
        scratch_shapes=[pltpu.VMEM((planes * ROWS, F * C), BF)],
        compiler_params=params(32),
        name="messages",
    )(table, *blocks)
    messages = messages[:1] + [
        lax.ppermute(messages[s], "tile", by_mate(s)) for s in range(1, GROUP)
    ]

    hidden, slope0, ocean = pl.pallas_call(
        first_kernel,
        out_shape=(shape(21 * C, PAIR), shape(21 * C, PAIR), shape(42 * C, C)),
        scratch_shapes=[pltpu.VMEM((22 * C, 2 * TAPS), BF)],
        compiler_params=params(48),
        name="first_layer",
        cost_estimate=pl.CostEstimate(flops=4 * 10**9, bytes_accessed=8 * MIB, transcendentals=10**6),
    )(ice_state, low, high, ocean_mask, weights[0], conv_bias)

    imitated, act0, grad1, project = pl.pallas_call(
        main_kernel,
        out_shape=(
            shape(ROWS, C, C),
            shape(17 * C, PAIR),
            shape(34 * C, C, dtype=F32),
            shape(F * ROWS, C),
        ),
        scratch_shapes=[
            pltpu.VMEM((EXT, FP, C), F32),
            pltpu.VMEM((EXT // GROUP * C, GROUP * C), F32),
            pltpu.VMEM((C, GROUP * C), BF),
            pltpu.VMEM((21 * C, 2 * TAPS), BF),
            pltpu.VMEM((20 * C, 2 * TAPS), BF),
            pltpu.VMEM((20 * C, PAIR), BF),
            pltpu.VMEM((19 * C, PAIR), BF),
            pltpu.VMEM((36 * C, C), F32),
            pltpu.VMEM((38 * C, C), BF),
            pltpu.VMEM((EXT // GROUP * C, C), BF),
        ],
        compiler_params=params(56),
        name="middle_layers",
        cost_estimate=pl.CostEstimate(flops=12 * 10**9, bytes_accessed=16 * MIB, transcendentals=10**6),
    )(
        *messages,
        col_map,
        lift_weight,
        conv_bias,
        hidden,
        slope0,
        ocean,
        sensitivity,
        low,
        high,
        weights[2],
        weights[4],
        weights[5],
        weights[3],
    )
    projects = [project] + [lax.ppermute(project, "tile", by_mate(s)) for s in range(1, GROUP)]

    state_grad = pl.pallas_call(
        last_kernel,
        out_shape=shape(ROWS, C, C),
        scratch_shapes=[pltpu.VMEM((17 * C, 2 * TAPS), BF)],
        compiler_params=params(48),
        name="last_adjoint",
        cost_estimate=pl.CostEstimate(flops=3 * 10**9, bytes_accessed=6 * MIB, transcendentals=0),
    )(act0, grad1, weights[1])

    sums = pl.pallas_call(
        functools.partial(scatter_kernel, planes),
        out_shape=tuple(shape(F * ROWS, C) for _ in range(planes)),
        scratch_shapes=[pltpu.VMEM((GROUP * ROWS, F * C), BF)],
        compiler_params=params(32),
        name="scatter",
    )(scatter, *projects)
    sums = [sums[0]] + [lax.ppermute(sums[z], "tile", by_plane(-z)) for z in range(1, planes)]
    panel_grad = pl.pallas_call(
        functools.partial(sum_kernel, planes),
        out_shape=shape(ROWS, F, C, dtype=F32),
        name="total",
    )(*sums)
    return imitated, state_grad, panel_grad.reshape(forcing.shape)


def solution(mesh):
    in_specs = (
        P(("member", "tile"), None, None, None),
        P(("member", "tile"), None, None),
        P(("member", "tile"), None, None),
        P("tile", None),
        P("tile", None),
        P("tile", None),
        P("tile", None),
        P(),
        P("tile", None),
        P(),
        P(),
        P(),
    )
    out_specs = (
        P(("member", "tile"), None, None),
        P(("member", "tile"), None, None),
        P(("member", "tile"), None, None, None),
    )
    return jax.shard_map(body, mesh=mesh, in_specs=in_specs, out_specs=out_specs, check_vma=False)
```

```python
import functools

import jax
import jax.numpy as jnp
from jax import lax
from jax.experimental import pallas as pl
from jax.experimental.pallas import tpu as pltpu
from jax.sharding import PartitionSpec as P

F = 10
FP = 16
K = 4
C = 128
ROWS = 32
EXT = 48
PAD = 8
GROUP = 8
SENT = GROUP // 2
PAIR = 2 * C
TAPS = 3 * C
BF = jnp.bfloat16
F32 = jnp.float32
MIB = 1 << 20


def params(mib):
    return pltpu.CompilerParams(vmem_limit_bytes=mib * MIB)


def dot(a, b, dims=(((1,), (0,)), ((), ()))):
    return lax.dot_general(a, b, dims, preferred_element_type=F32)


def split(x):
    high = x.astype(BF)
    return high, (x - high.astype(F32)).astype(BF)


def fine_dot(a, b, dims=(((1,), (0,)), ((), ()))):
    ah, al = split(a)
    bh, bl = split(b)
    return dot(ah, bh, dims) + (dot(ah, bl, dims) + dot(al, bh, dims))


def pair_rows(index, count=1):
    start = index * C
    if not isinstance(index, int):
        start = pl.multiple_of(start, C)
    return pl.ds(start, count * C)


def store_pair(xp, index, value):
    column = lax.broadcasted_iota(jnp.int32, (C, PAIR), 0)
    before = jnp.where(column == 0, 0.0, pltpu.roll(value, 1, 0)).astype(BF)
    after = jnp.where(column == C - 1, 0.0, pltpu.roll(value, C - 1, 0)).astype(BF)
    value = value.astype(BF)
    rows = pair_rows(index)
    for half in range(2):
        lanes = slice(half * C, half * C + C)
        for tap, part in enumerate((before, value, after)):
            start = half * TAPS + tap * C
            xp[rows, start : start + C] = part[:, lanes]


def centre(xp, index):
    low = xp[pair_rows(index), TAPS + C : TAPS + 2 * C]
    high = xp[pair_rows(index + 1), C : 2 * C]
    return jnp.concatenate([low, high], axis=1).astype(F32)


def two_rows(ref, row):
    start = row * C
    if not isinstance(row, int):
        start = pl.multiple_of(start, C)
    low = ref[pl.ds(start, C), :]
    high = ref[pl.ds(start + C, C), :]
    return jnp.concatenate([low, high], axis=1).astype(F32)


def layer(xp, weight, count, step, finish):
    for first in range(0, count, step):
        size = min(step, count - first)
        total = dot(xp[pair_rows(first, size), :], weight[: 2 * TAPS, :])
        total += dot(xp[pair_rows(first + 1, size), :], weight[2 * TAPS :, :])
        for j in range(size):
            finish(first + j, total[j * C : (j + 1) * C])


def by_field(value, field):
    panels = value.shape[0] // (F * 8)
    part = value.reshape(panels, F, 8, C)[:, field]
    return part.reshape(panels * 8, C)


def column_tables(table, devices):
    entries = [table[jnp.clip(device, 0, table.shape[0] - 1)] for device in devices]
    fill = jnp.zeros((C - 2 * K * len(entries), C), F32)
    return jnp.concatenate(entries + [fill], axis=0).T


def picked(columns, place, ident, start, size):
    total = jnp.zeros((size, ident.shape[1]), F32)
    part = columns[start : start + size]
    for k in range(K):
        at = place * 2 * K + k
        total += jnp.where(part[:, at : at + 1] == ident, part[:, at + K : at + K + 1], 0.0)
    return total


def source_ident(planes, plane, spot, sides):
    lane = lax.broadcasted_iota(jnp.int32, (1, sides * planes * ROWS), 1)
    from_plane = lax.rem(plane - (lane // ROWS) % planes + planes, planes)
    from_spot = jnp.where(lane < planes * ROWS, spot, spot ^ 1)
    return ((from_plane * GROUP + from_spot) * ROWS + lane % ROWS).astype(F32)


def pick_kernel(planes, table, picks, scatter):
    me = lax.axis_index("tile")
    plane, spot = me // GROUP, me % GROUP
    count = planes * GROUP
    ident = source_ident(planes, plane, spot, 2)
    devices = [plane * GROUP + (spot ^ s) + step for s in range(0, GROUP, 2) for step in (-1, 0, 1)]
    columns = column_tables(table, devices)
    parts = []
    for place, device in enumerate(devices):
        start, size = ((ROWS - PAD, PAD), (0, ROWS), (0, PAD))[place % 3]
        inside = jnp.logical_and(device >= 0, device < count)
        parts.append(jnp.where(inside, picked(columns, place, ident, start, size), 0.0))
    picks[...] = jnp.concatenate(parts, axis=0).astype(BF)
    ident = source_ident(planes, plane, spot, 1)
    columns = column_tables(table, [plane * GROUP + (spot ^ s) for s in range(GROUP)])
    parts = [picked(columns, s, ident, 0, ROWS) for s in range(GROUP)]
    scatter[...] = jnp.concatenate(parts, axis=0).T.astype(BF)


def message_kernel(planes, picks, own, mate, *refs):
    outs, wide = refs[:-1], refs[-1]
    sources = planes * ROWS
    for side, block in enumerate((own, mate)):
        value = block[...].astype(F32)
        for f in range(F):
            wide[side * sources : (side + 1) * sources, f * C : (f + 1) * C] = by_field(
                value, f
            ).astype(BF)
    for f in range(F):
        found = dot(picks[...], wide[:, f * C : (f + 1) * C]).astype(BF)
        for n, out in enumerate(outs):
            out[f * EXT : (f + 1) * EXT, :] = found[n * EXT : (n + 1) * EXT]


def fill_taps(taps, weight, l, back):
    zero = jnp.zeros((TAPS, C), BF)
    taps[0:TAPS, C:] = zero
    taps[3 * TAPS :, :C] = zero
    for a in range(3):
        for b in range(3):
            if back:
                block = weight[l, 2 - a, 2 - b].astype(F32).T.astype(BF)
            else:
                block = weight[l, a, b]
            for half in range(2):
                start = (a + half) * TAPS + b * C
                taps[start : start + C, half * C : half * C + C] = block


def first_kernel(ice, low, high, mask, weight, bias, hidden, slope, ocean, xp, taps):
    fill_taps(taps, weight, 0, False)

    def ice_row(r):
        if r < 0:
            return low[r + 6]
        if r >= ROWS:
            return high[r - ROWS]
        return ice[r]

    for p in range(22):
        row = 2 * p - 6
        store_pair(xp, p, jnp.concatenate([ice_row(row), ice_row(row + 1)], axis=1).astype(F32))
    before = low[9, 0:ROWS, :].astype(F32)[ROWS - PAD :]
    after = high[9, 0:ROWS, :].astype(F32)[:PAD]
    cells = jnp.concatenate([before, mask[...].astype(F32), after], axis=0)
    cells = jnp.concatenate([cells, jnp.zeros((C - EXT, C), F32)], axis=0).T
    for r in range(-5, 37):
        column = jnp.broadcast_to(cells[:, r + PAD : r + PAD + 1], (C, C))
        ocean[(r + 5) * C : (r + 6) * C, :] = column.astype(BF)
    both = jnp.concatenate([bias[0:1, :], bias[0:1, :]], axis=1)

    def finish(p, total):
        tangent = jnp.tanh(total + both)
        cell = two_rows(ocean, 2 * p)
        moved = cell * tangent
        slope[pair_rows(p), :] = (cell - moved * tangent).astype(BF)
        hidden[pair_rows(p), :] = (centre(xp, p) + moved).astype(BF)

    layer(xp, taps, 21, 4, finish)


def main_kernel(*refs):
    messages = refs[:SENT]
    (col_map, lift, bias, hidden, slope0, ocean, sens, low, high, weight) = refs[SENT : SENT + 10]
    imitated, act0, grad1, project = refs[SENT + 10 : SENT + 14]
    ice, lifted, diag, xa, xb, slope1, slope2, grads, out_rows, turned, *taps = refs[SENT + 14 :]
    w1f, w2f, w2b, w1b = taps
    for n, (l, back) in enumerate(((1, False), (2, False), (2, True), (1, True))):
        fill_taps(taps[n], weight, l, back)
    ice[...] = jnp.zeros(ice.shape, F32)
    for f in range(F):
        rows = slice(f * EXT, (f + 1) * EXT)
        total = messages[0][rows, :].astype(F32)
        for s in range(1, SENT):
            total += messages[s][rows, :].astype(F32)
        ice[:, f, :] = fine_dot(total, col_map[...])
    diag[...] = jnp.zeros(diag.shape, BF)
    for j in range(GROUP):
        diag[j * FP : j * FP + F, j * C : (j + 1) * C] = lift[...]
    for group in range(EXT // GROUP):
        block = ice[group * GROUP : (group + 1) * GROUP].reshape(C, C)
        turned[group * C : (group + 1) * C, :] = block.T.astype(BF)
    for group in range(EXT // GROUP):
        lifted[group * C : (group + 1) * C, :] = dot(
            turned[group * C : (group + 1) * C, :], diag[...]
        )

    def lifted_row(r):
        e = r + PAD
        return lifted[(e // 8) * C : (e // 8 + 1) * C, (e % 8) * C : (e % 8 + 1) * C]

    for p in range(21):
        row = 2 * p - 5
        add = jnp.concatenate([lifted_row(row), lifted_row(row + 1)], axis=1)
        value = (hidden[pair_rows(p), :].astype(F32) + add).astype(BF)
        store_pair(xa, p, value.astype(F32))

    def bias_of(l):
        return jnp.concatenate([bias[l : l + 1, :], bias[l : l + 1, :]], axis=1)

    bias1, bias2 = bias_of(1), bias_of(2)

    def finish1(p, total):
        tangent = jnp.tanh(total + bias1)
        cell = two_rows(ocean, 2 * p + 1)
        moved = cell * tangent
        slope1[pair_rows(p), :] = (cell - moved * tangent).astype(BF)
        value = (centre(xa, p) + moved).astype(BF)
        store_pair(xb, p, value.astype(F32))

    layer(xa, w1f, 20, 4, finish1)

    def finish2(p, total):
        tangent = jnp.tanh(total + bias2)
        cell = two_rows(ocean, 2 * p + 2)
        moved = cell * tangent
        slope2[pair_rows(p), :] = (cell - moved * tangent).astype(BF)
        value = (centre(xb, p) + moved).astype(BF)
        out_rows[pair_rows(2 * p), :] = value[:, :C]
        out_rows[pair_rows(2 * p + 1), :] = value[:, C:]

    layer(xb, w2f, 19, 4, finish2)
    imitated[...] = out_rows[3 * C : 35 * C, :].reshape(ROWS, C, C)

    def sens_row(r):
        if r < 0:
            return low[r + 9]
        if r >= ROWS:
            return high[r - ROWS + 6]
        return sens[r]

    for p in range(19):
        row = 2 * p - 3
        value = jnp.concatenate([sens_row(row), sens_row(row + 1)], axis=1).astype(F32)
        store_pair(xa, p, value * slope2[pair_rows(p), :].astype(F32))
        out_rows[pair_rows(2 * p), :] = sens_row(row)
        out_rows[pair_rows(2 * p + 1), :] = sens_row(row + 1)

    def finish3(p, total):
        total += two_rows(out_rows, 2 * p + 1)
        grads[pair_rows(2 * p), :] = total[:, :C]
        grads[pair_rows(2 * p + 1), :] = total[:, C:]
        store_pair(xb, p, total * slope1[pair_rows(p + 1), :].astype(F32))

    layer(xa, w2b, 18, 4, finish3)

    def finish4(p, total):
        total += two_rows(grads, 2 * p + 1)
        act0[pair_rows(p), :] = (total * slope0[pair_rows(p + 2), :].astype(F32)).astype(BF)
        grad1[pair_rows(2 * p), :] = total[:, :C]
        grad1[pair_rows(2 * p + 1), :] = total[:, C:]

    layer(xb, w1b, 17, 4, finish4)
    short = jnp.concatenate([lift[...].astype(F32), jnp.zeros((FP - F, C), F32)], axis=0).astype(BF)
    nt = (((1,), (1,)), ((), ()))
    for r in range(ROWS):
        part = dot(short, grad1[(r + 1) * C : (r + 2) * C, :].astype(BF), nt)
        ice[r, :, :] = part
    ice[0:ROWS] = fine_dot(ice[0:ROWS].reshape(ROWS * FP, C), col_map[...], nt).reshape(ROWS, FP, C)
    for f in range(F):
        project[f * ROWS : (f + 1) * ROWS, :] = ice[0:ROWS, f, :].astype(BF)


def last_kernel(act0, grad1, weight, out, xp, taps):
    fill_taps(taps, weight, 0, True)
    for p in range(17):
        store_pair(xp, p, act0[pair_rows(p), :].astype(F32))

    def finish(p, total):
        total += two_rows(grad1, 2 * p + 1)
        out[2 * p] = total[:, :C].astype(BF)
        out[2 * p + 1] = total[:, C:].astype(BF)

    layer(xp, taps, 16, 4, finish)


def scatter_kernel(planes, scatter, own, mate, *refs):
    outs, wide, found = refs[:-2], refs[-2], refs[-1]
    for s in range(GROUP):
        block, row = (own, mate)[s % 2], (s // 2) * F * ROWS
        for f in range(F):
            wide[s * ROWS : (s + 1) * ROWS, f * C : (f + 1) * C] = block[
                row + f * ROWS : row + (f + 1) * ROWS, :
            ]
    for f in range(F):
        part = dot(scatter[...], wide[:, f * C : (f + 1) * C])
        for panel in range(planes * ROWS // 8):
            row = (panel * F + f) * 8
            found[row : row + 8, :] = part[panel * 8 : panel * 8 + 8]
    for z in range(planes):
        outs[z][...] = found[z * F * ROWS : (z + 1) * F * ROWS, :].astype(BF)


def shape(*dims, dtype=BF):
    return jax.ShapeDtypeStruct(dims, dtype)


def body(
    forcing,
    ice_state,
    sensitivity,
    owner_device,
    panel_slot,
    row_offset,
    intersection_weight,
    col_map,
    ocean_mask,
    lift_weight,
    conv_weight,
    conv_bias,
):
    count = lax.axis_size("tile")
    planes = count // GROUP

    def by_plane(step):
        return [(i, (i + GROUP * step) % count) for i in range(count)]

    def by_mate(step):
        return [(i, i ^ step) for i in range(count)]

    fields = forcing.transpose(0, 2, 1, 3).reshape(F * ROWS, C)
    blocks = [fields] + [lax.ppermute(fields, "tile", by_plane(z)) for z in range(1, planes)]

    ident = (owner_device * 4 + panel_slot) * 8 + row_offset
    table = jnp.concatenate([ident.T.astype(F32), intersection_weight.T], axis=0)
    table = jnp.pad(table, ((0, 0), (0, C - ROWS)))
    table = jnp.broadcast_to(table[None], (count, 2 * K, C))
    ready = table
    table = lax.all_to_all(table, "tile", 0, 0, tiled=True)
    own_column = jnp.concatenate(blocks, axis=0)
    mate_column = lax.ppermute(own_column, "tile", by_mate(1))

    cells = jnp.pad(ocean_mask, ((0, C - ROWS), (0, 0)))[None].astype(BF)
    to_next = jnp.concatenate([ice_state[ROWS - 6 :], sensitivity[ROWS - 3 :], cells], axis=0)
    to_last = jnp.concatenate([ice_state[:6], sensitivity[:3], cells], axis=0)
    picks, scatter = pl.pallas_call(
        functools.partial(pick_kernel, planes),
        out_shape=(shape(SENT * EXT, 2 * planes * ROWS), shape(planes * ROWS, GROUP * ROWS)),
        compiler_params=params(4),
        name="picks",
        cost_estimate=pl.CostEstimate(flops=10**10, bytes_accessed=MIB, transcendentals=0),
    )(table)
    messages = pl.pallas_call(
        functools.partial(message_kernel, planes),
        out_shape=tuple(shape(F * EXT, C) for _ in range(SENT)),
        scratch_shapes=[pltpu.VMEM((2 * planes * ROWS, F * C), BF)],
        compiler_params=params(10),
        name="messages",
    )(picks, own_column, mate_column)
    to_next, to_last, _ = lax.optimization_barrier((to_next, to_last, ready))
    forward = [(i, i + 1) for i in range(count - 1)]
    low = lax.ppermute(to_next, "tile", forward)
    high = lax.ppermute(to_last, "tile", [(b, a) for a, b in forward])
    messages = [messages[0]] + [
        lax.ppermute(messages[s], "tile", by_mate(2 * s)) for s in range(1, SENT)
    ]
    hidden, slope0, ocean = pl.pallas_call(
        first_kernel,
        out_shape=(shape(21 * C, PAIR), shape(21 * C, PAIR), shape(42 * C, C)),
        scratch_shapes=[pltpu.VMEM((22 * C, 2 * TAPS), BF), pltpu.VMEM((4 * TAPS, PAIR), BF)],
        compiler_params=params(14),
        name="first_layer",
        cost_estimate=pl.CostEstimate(flops=4 * 10**9, bytes_accessed=8 * MIB, transcendentals=10**6),
    )(ice_state, low, high, ocean_mask, conv_weight, conv_bias)

    imitated, act0, grad1, project = pl.pallas_call(
        main_kernel,
        out_shape=(
            shape(ROWS, C, C),
            shape(17 * C, PAIR),
            shape(34 * C, C, dtype=F32),
            shape(F * ROWS, C),
        ),
        scratch_shapes=[
            pltpu.VMEM((EXT, FP, C), F32),
            pltpu.VMEM((EXT // GROUP * C, GROUP * C), F32),
            pltpu.VMEM((C, GROUP * C), BF),
            pltpu.VMEM((21 * C, 2 * TAPS), BF),
            pltpu.VMEM((20 * C, 2 * TAPS), BF),
            pltpu.VMEM((20 * C, PAIR), BF),
            pltpu.VMEM((19 * C, PAIR), BF),
            pltpu.VMEM((36 * C, C), F32),
            pltpu.VMEM((38 * C, C), BF),
            pltpu.VMEM((EXT // GROUP * C, C), BF),
        ]
        + [pltpu.VMEM((4 * TAPS, PAIR), BF)] * 4,
        compiler_params=params(32),
        name="middle_layers",
        cost_estimate=pl.CostEstimate(flops=12 * 10**9, bytes_accessed=16 * MIB, transcendentals=10**6),
    )(
        *messages,
        col_map,
        lift_weight,
        conv_bias,
        hidden,
        slope0,
        ocean,
        sensitivity,
        low,
        high,
        conv_weight,
    )
    projects = [project] + [lax.ppermute(project, "tile", by_mate(2 * s)) for s in range(1, SENT)]
    own_projects = jnp.concatenate(projects, axis=0)
    mate_projects = lax.ppermute(own_projects, "tile", by_mate(1))

    sums = pl.pallas_call(
        functools.partial(scatter_kernel, planes),
        out_shape=tuple(shape(F * ROWS, C) for _ in range(planes)),
        scratch_shapes=[
            pltpu.VMEM((GROUP * ROWS, F * C), BF),
            pltpu.VMEM((planes * F * ROWS, C), F32),
        ],
        compiler_params=params(8),
        name="scatter",
    )(scatter, own_projects, mate_projects)
    act0, *sums = lax.optimization_barrier((act0, *sums))
    sums = [sums[0]] + [lax.ppermute(sums[z], "tile", by_plane(-z)) for z in range(1, planes)]
    state_grad = pl.pallas_call(
        last_kernel,
        out_shape=shape(ROWS, C, C),
        scratch_shapes=[pltpu.VMEM((17 * C, 2 * TAPS), BF), pltpu.VMEM((4 * TAPS, PAIR), BF)],
        compiler_params=params(14),
        name="last_adjoint",
        cost_estimate=pl.CostEstimate(flops=3 * 10**9, bytes_accessed=6 * MIB, transcendentals=0),
    )(act0, grad1, conv_weight)

    panel_grad = sum(block.astype(F32) for block in sums)
    panels = forcing.shape[0]
    panel_grad = panel_grad.reshape(panels, F, 8, C).transpose(0, 2, 1, 3)
    return imitated, state_grad, panel_grad


def solution(mesh):
    in_specs = (
        P(("member", "tile"), None, None, None),
        P(("member", "tile"), None, None),
        P(("member", "tile"), None, None),
        P("tile", None),
        P("tile", None),
        P("tile", None),
        P("tile", None),
        P(),
        P("tile", None),
        P(),
        P(),
        P(),
    )
    out_specs = (
        P(("member", "tile"), None, None),
        P(("member", "tile"), None, None),
        P(("member", "tile"), None, None, None),
    )
    return jax.shard_map(body, mesh=mesh, in_specs=in_specs, out_specs=out_specs, check_vma=False)
```

```python
import functools

import jax
import jax.numpy as jnp
from jax import lax
from jax.experimental import pallas as pl
from jax.experimental.pallas import tpu as pltpu
from jax.sharding import PartitionSpec as P

F = 10
FP = 16
K = 4
C = 128
ROWS = 32
EXT = 48
PAD = 8
GROUP = 8
SENT = GROUP // 2
STEP = 1
PAIR = 2 * C
BF = jnp.bfloat16
F32 = jnp.float32
MIB = 1 << 20


def params(mib):
    return pltpu.CompilerParams(vmem_limit_bytes=mib * MIB)


def dot(a, b, dims=(((1,), (0,)), ((), ()))):
    return lax.dot_general(a, b, dims, preferred_element_type=F32)


def split(x):
    high = x.astype(BF)
    return high, (x - high.astype(F32)).astype(BF)


def fine_dot(a, b, dims=(((1,), (0,)), ((), ()))):
    ah, al = split(a)
    bh, bl = split(b)
    return dot(ah, bh, dims) + (dot(ah, bl, dims) + dot(al, bh, dims))


def pair_rows(index, count=1):
    start = index * C
    if not isinstance(index, int):
        start = pl.multiple_of(start, C)
    return pl.ds(start, count * C)


def store_pair(xp, index, value):
    xp[pair_rows(index), :] = value.astype(BF)


def centre(xp, index):
    low = xp[pair_rows(index), C:]
    high = xp[pair_rows(index + 1), :C]
    return jnp.concatenate([low, high], axis=1).astype(F32)


def two_rows(ref, row):
    start = row * C
    if not isinstance(row, int):
        start = pl.multiple_of(start, C)
    low = ref[pl.ds(start, C), :]
    high = ref[pl.ds(start + C, C), :]
    return jnp.concatenate([low, high], axis=1).astype(F32)


def layer(xp, taps, count, step, finish):
    sub_row = lax.broadcasted_iota(jnp.int32, (8, PAIR), 0)
    for first in range(0, count, step):
        size = min(step, count - first)
        seen = jnp.concatenate(
            [xp[pair_rows(first, size), :], xp[pair_rows(first + 1, size), :]], axis=1
        )
        parts = [dot(seen, taps[:, b * PAIR : (b + 1) * PAIR]) for b in range(3)]
        for j in range(size):
            rows = slice(j * C, (j + 1) * C)
            before = pltpu.roll(parts[0][rows], 1, 0)
            before = jnp.concatenate([jnp.where(sub_row == 0, 0.0, before[:8]), before[8:]], axis=0)
            after = pltpu.roll(parts[2][rows], C - 1, 0)
            after = jnp.concatenate([after[:-8], jnp.where(sub_row == 7, 0.0, after[-8:])], axis=0)
            finish(first + j, parts[1][rows] + before + after)


def by_field(value, field):
    panels = value.shape[0] // (F * 8)
    part = value.reshape(panels, F, 8, C)[:, field]
    return part.reshape(panels * 8, C)


def column_tables(table, devices):
    entries = [table[jnp.clip(device, 0, table.shape[0] - 1)] for device in devices]
    fill = jnp.zeros((C - 2 * K * len(entries), C), F32)
    return jnp.concatenate(entries + [fill], axis=0).T


def picked(columns, place, ident, start, size):
    total = jnp.zeros((size, ident.shape[1]), F32)
    part = columns[start : start + size]
    for k in range(K):
        at = place * 2 * K + k
        total += jnp.where(part[:, at : at + 1] == ident, part[:, at + K : at + K + 1], 0.0)
    return total


def source_ident(planes, plane, spot, sides):
    lane = lax.broadcasted_iota(jnp.int32, (1, sides * planes * ROWS), 1)
    from_plane = lax.rem(plane - (lane // ROWS) % planes + planes, planes)
    from_spot = jnp.where(lane < planes * ROWS, spot, spot ^ 1)
    return ((from_plane * GROUP + from_spot) * ROWS + lane % ROWS).astype(F32)


def pick_kernel(planes, table, picks, scatter):
    me = lax.axis_index("tile")
    plane, spot = me // GROUP, me % GROUP
    count = planes * GROUP
    ident = source_ident(planes, plane, spot, 2)
    devices = [plane * GROUP + (spot ^ s) + step for s in range(0, GROUP, 2) for step in (-1, 0, 1)]
    columns = column_tables(table, devices)
    parts = []
    for place, device in enumerate(devices):
        start, size = ((ROWS - PAD, PAD), (0, ROWS), (0, PAD))[place % 3]
        inside = jnp.logical_and(device >= 0, device < count)
        parts.append(jnp.where(inside, picked(columns, place, ident, start, size), 0.0))
    picks[...] = jnp.concatenate(parts, axis=0).astype(BF)
    ident = source_ident(planes, plane, spot, 1)
    columns = column_tables(table, [plane * GROUP + (spot ^ s) for s in range(GROUP)])
    parts = [picked(columns, s, ident, 0, ROWS) for s in range(GROUP)]
    scatter[...] = jnp.concatenate(parts, axis=0).T.astype(BF)


def message_kernel(planes, picks, own, mate, *refs):
    outs, wide = refs[:-1], refs[-1]
    sources = planes * ROWS
    for side, block in enumerate((own, mate)):
        value = block[...].astype(F32)
        for f in range(F):
            wide[side * sources : (side + 1) * sources, f * C : (f + 1) * C] = by_field(
                value, f
            ).astype(BF)
    for f in range(F):
        found = dot(picks[...], wide[:, f * C : (f + 1) * C]).astype(BF)
        for n, out in enumerate(outs):
            out[f * EXT : (f + 1) * EXT, :] = found[n * EXT : (n + 1) * EXT]


def fill_taps(taps, weight, l, back):
    zero = jnp.zeros((C, C), BF)
    for b in range(3):
        taps[0:C, b * PAIR + C : (b + 1) * PAIR] = zero
        taps[3 * C :, b * PAIR : b * PAIR + C] = zero
        for a in range(3):
            if back:
                block = weight[l, 2 - a, 2 - b].astype(F32).T.astype(BF)
            else:
                block = weight[l, a, b]
            for half in range(2):
                start = b * PAIR + half * C
                taps[(a + half) * C : (a + half + 1) * C, start : start + C] = block


def first_kernel(ice, low, high, mask, weight, bias, hidden, slope, ocean, xp, taps):
    fill_taps(taps, weight, 0, False)

    def ice_row(r):
        if r < 0:
            return low[(r + 6) * C : (r + 7) * C, :]
        if r >= ROWS:
            return high[(r - ROWS) * C : (r - ROWS + 1) * C, :]
        return ice[r]

    for p in range(22):
        row = 2 * p - 6
        store_pair(xp, p, jnp.concatenate([ice_row(row), ice_row(row + 1)], axis=1).astype(F32))
    before = low[9 * C : 9 * C + 2 * PAD, :].astype(F32)[:PAD]
    after = high[9 * C : 9 * C + 2 * PAD, :].astype(F32)[:PAD]
    cells = jnp.concatenate([before, mask[...].astype(F32), after], axis=0)
    cells = jnp.concatenate([cells, jnp.zeros((C - EXT, C), F32)], axis=0).T
    for r in range(-5, 37):
        column = jnp.broadcast_to(cells[:, r + PAD : r + PAD + 1], (C, C))
        ocean[(r + 5) * C : (r + 6) * C, :] = column.astype(BF)
    both = jnp.concatenate([bias[0:1, :], bias[0:1, :]], axis=1)

    def finish(p, total):
        tangent = jnp.tanh(total + both)
        cell = two_rows(ocean, 2 * p)
        moved = cell * tangent
        slope[pair_rows(p), :] = (cell - moved * tangent).astype(BF)
        hidden[pair_rows(p), :] = (centre(xp, p) + moved).astype(BF)

    layer(xp, taps, 21, STEP, finish)


def main_kernel(*refs):
    messages = refs[:SENT]
    (col_map, lift, bias, hidden, slope0, ocean, sens, low, high, weight) = refs[SENT : SENT + 10]
    imitated, act0, grad1, project = refs[SENT + 10 : SENT + 14]
    ice, lifted, diag, xa, xb, slope1, slope2, grads, out_rows, turned, shown, sem, *taps = refs[SENT + 14 :]
    w1f, w2f, w2b, w1b = taps
    for n, (l, back) in enumerate(((1, False), (2, False), (2, True), (1, True))):
        fill_taps(taps[n], weight, l, back)
    ice[...] = jnp.zeros(ice.shape, F32)
    for f in range(F):
        rows = slice(f * EXT, (f + 1) * EXT)
        total = messages[0][rows, :].astype(F32)
        for s in range(1, SENT):
            total += messages[s][rows, :].astype(F32)
        ice[:, f, :] = fine_dot(total, col_map[...])
    diag[...] = jnp.zeros(diag.shape, BF)
    for j in range(GROUP):
        diag[j * FP : j * FP + F, j * C : (j + 1) * C] = lift[...]
    for group in range(EXT // GROUP):
        block = ice[group * GROUP : (group + 1) * GROUP].reshape(C, C)
        turned[group * C : (group + 1) * C, :] = block.T.astype(BF)
    for group in range(EXT // GROUP):
        lifted[group * C : (group + 1) * C, :] = dot(
            turned[group * C : (group + 1) * C, :], diag[...]
        )

    def lifted_row(r):
        e = r + PAD
        return lifted[(e // 8) * C : (e // 8 + 1) * C, (e % 8) * C : (e % 8 + 1) * C]

    for p in range(21):
        row = 2 * p - 5
        add = jnp.concatenate([lifted_row(row), lifted_row(row + 1)], axis=1)
        store_pair(xa, p, hidden[pair_rows(p), :].astype(F32) + add)

    def bias_of(l):
        return jnp.concatenate([bias[l : l + 1, :], bias[l : l + 1, :]], axis=1)

    bias1, bias2 = bias_of(1), bias_of(2)

    def finish1(p, total):
        tangent = jnp.tanh(total + bias1)
        cell = two_rows(ocean, 2 * p + 1)
        moved = cell * tangent
        slope1[pair_rows(p), :] = (cell - moved * tangent).astype(BF)
        store_pair(xb, p, centre(xa, p) + moved)

    layer(xa, w1f, 20, STEP, finish1)

    def finish2(p, total):
        tangent = jnp.tanh(total + bias2)
        cell = two_rows(ocean, 2 * p + 2)
        moved = cell * tangent
        slope2[pair_rows(p), :] = (cell - moved * tangent).astype(BF)
        value = (centre(xb, p) + moved).astype(BF)
        for half in range(2):
            row = 2 * p + half - 3
            if 0 <= row < ROWS:
                shown[row] = value[:, half * C : half * C + C]

    layer(xb, w2f, 19, STEP, finish2)
    copy = pltpu.make_async_copy(shown, imitated, sem)
    copy.start()

    def sens_row(r):
        if r < 0:
            return low[(r + 9) * C : (r + 10) * C, :]
        if r >= ROWS:
            return high[(r - ROWS + 6) * C : (r - ROWS + 7) * C, :]
        return sens[r]

    for p in range(19):
        row = 2 * p - 3
        value = jnp.concatenate([sens_row(row), sens_row(row + 1)], axis=1).astype(F32)
        store_pair(xa, p, value * slope2[pair_rows(p), :].astype(F32))
        out_rows[pair_rows(2 * p), :] = sens_row(row)
        out_rows[pair_rows(2 * p + 1), :] = sens_row(row + 1)

    def finish3(p, total):
        total += two_rows(out_rows, 2 * p + 1)
        grads[pair_rows(2 * p), :] = total[:, :C]
        grads[pair_rows(2 * p + 1), :] = total[:, C:]
        store_pair(xb, p, total * slope1[pair_rows(p + 1), :].astype(F32))

    layer(xa, w2b, 18, STEP, finish3)

    def finish4(p, total):
        total += two_rows(grads, 2 * p + 1)
        act0[pair_rows(p), :] = (total * slope0[pair_rows(p + 2), :].astype(F32)).astype(BF)
        grad1[pair_rows(2 * p), :] = total[:, :C]
        grad1[pair_rows(2 * p + 1), :] = total[:, C:]

    layer(xb, w1b, 17, STEP, finish4)
    short = jnp.concatenate([lift[...].astype(F32), jnp.zeros((FP - F, C), F32)], axis=0).astype(BF)
    nt = (((1,), (1,)), ((), ()))
    for r in range(ROWS):
        part = dot(short, grad1[(r + 1) * C : (r + 2) * C, :].astype(BF), nt)
        ice[r, :, :] = part
    ice[0:ROWS] = fine_dot(ice[0:ROWS].reshape(ROWS * FP, C), col_map[...], nt).reshape(ROWS, FP, C)
    for f in range(F):
        project[f * ROWS : (f + 1) * ROWS, :] = ice[0:ROWS, f, :].astype(BF)
    copy.wait()


def last_kernel(act0, grad1, weight, out, xp, taps):
    fill_taps(taps, weight, 0, True)
    for p in range(17):
        store_pair(xp, p, act0[pair_rows(p), :].astype(F32))

    def finish(p, total):
        total += two_rows(grad1, 2 * p + 1)
        out[2 * p] = total[:, :C].astype(BF)
        out[2 * p + 1] = total[:, C:].astype(BF)

    layer(xp, taps, 16, STEP, finish)


def scatter_kernel(planes, scatter, own, mate, *refs):
    outs, wide, found = refs[:-2], refs[-2], refs[-1]
    for s in range(GROUP):
        block, row = (own, mate)[s % 2], (s // 2) * F * ROWS
        for f in range(F):
            wide[s * ROWS : (s + 1) * ROWS, f * C : (f + 1) * C] = block[
                row + f * ROWS : row + (f + 1) * ROWS, :
            ]
    for f in range(F):
        part = dot(scatter[...], wide[:, f * C : (f + 1) * C])
        for panel in range(planes * ROWS // 8):
            row = (panel * F + f) * 8
            found[row : row + 8, :] = part[panel * 8 : panel * 8 + 8]
    for z in range(planes):
        outs[z][...] = found[z * F * ROWS : (z + 1) * F * ROWS, :].astype(BF)


def shape(*dims, dtype=BF):
    return jax.ShapeDtypeStruct(dims, dtype)


def body(
    forcing,
    ice_state,
    sensitivity,
    owner_device,
    panel_slot,
    row_offset,
    intersection_weight,
    col_map,
    ocean_mask,
    lift_weight,
    conv_weight,
    conv_bias,
):
    count = lax.axis_size("tile")
    planes = count // GROUP

    def by_plane(step):
        return [(i, (i + GROUP * step) % count) for i in range(count)]

    def by_mate(step):
        return [(i, i ^ step) for i in range(count)]

    def spread(array, above):
        array = jnp.pad(array.T, ((K * above, K - K * above), (0, C - ROWS)))
        return jnp.broadcast_to(array[None], (count, 2 * K, C))

    ident = (spread(owner_device, 0) * 4 + spread(panel_slot, 0)) * 8 + spread(row_offset, 0)
    table = ident.astype(F32) + spread(intersection_weight, 1)
    ready = table
    table = lax.all_to_all(table, "tile", 0, 0, tiled=True)
    fields = forcing.transpose(0, 2, 1, 3).reshape(F * ROWS, C)
    blocks = [fields] + [lax.ppermute(fields, "tile", by_plane(z)) for z in range(1, planes)]
    own_column = jnp.concatenate(blocks, axis=0)
    mate_column = lax.ppermute(own_column, "tile", by_mate(1))

    rows_sent = 9 * C + 2 * PAD

    def window(array, start, size, place):
        array = lax.slice_in_dim(array, start, start + size)
        return jnp.pad(array, ((place, rows_sent - place - size), (0, 0)))

    def edge(arrays, ice_row, sens_row, mask_row):
        ice, sens, mask = arrays
        return (
            window(ice.reshape(ROWS * C, C), ice_row * C, 6 * C, 0)
            + window(sens.reshape(ROWS * C, C), sens_row * C, 3 * C, 6 * C)
            + jnp.where(window(mask, mask_row, PAD, 9 * C) == 1, 1.0, 0.0).astype(BF)
        )

    arrays = (ice_state, sensitivity, ocean_mask)
    to_next = edge(arrays, ROWS - 6, ROWS - 3, ROWS - PAD)
    to_last = edge(lax.optimization_barrier(arrays), 0, 0, 0)
    picks, scatter = pl.pallas_call(
        functools.partial(pick_kernel, planes),
        out_shape=(shape(SENT * EXT, 2 * planes * ROWS), shape(planes * ROWS, GROUP * ROWS)),
        compiler_params=params(4),
        name="picks",
        cost_estimate=pl.CostEstimate(flops=10**10, bytes_accessed=MIB, transcendentals=0),
    )(table)
    messages = pl.pallas_call(
        functools.partial(message_kernel, planes),
        out_shape=tuple(shape(F * EXT, C) for _ in range(SENT)),
        scratch_shapes=[pltpu.VMEM((2 * planes * ROWS, F * C), BF)],
        compiler_params=params(10),
        name="messages",
    )(picks, own_column, mate_column)
    to_next, to_last, _ = lax.optimization_barrier((to_next, to_last, ready))
    forward = [(i, i + 1) for i in range(count - 1)]
    low = lax.ppermute(to_next, "tile", forward)
    high = lax.ppermute(to_last, "tile", [(b, a) for a, b in forward])
    messages = [messages[0]] + [
        lax.ppermute(messages[s], "tile", by_mate(2 * s)) for s in range(1, SENT)
    ]
    hidden, slope0, ocean = pl.pallas_call(
        first_kernel,
        out_shape=(shape(21 * C, PAIR), shape(21 * C, PAIR), shape(42 * C, C)),
        scratch_shapes=[pltpu.VMEM((22 * C, PAIR), BF), pltpu.VMEM((4 * C, 3 * PAIR), BF)],
        compiler_params=params(14),
        name="first_layer",
        cost_estimate=pl.CostEstimate(flops=4 * 10**9, bytes_accessed=8 * MIB, transcendentals=10**6),
    )(ice_state, low, high, ocean_mask, conv_weight, conv_bias)

    imitated, act0, grad1, project = pl.pallas_call(
        main_kernel,
        out_shape=(
            shape(ROWS, C, C),
            shape(17 * C, PAIR),
            shape(34 * C, C, dtype=F32),
            shape(F * ROWS, C),
        ),
        out_specs=(pl.BlockSpec(memory_space=pltpu.HBM),)
        + (pl.BlockSpec(memory_space=pltpu.VMEM),) * 3,
        scratch_shapes=[
            pltpu.VMEM((EXT, FP, C), F32),
            pltpu.VMEM((EXT // GROUP * C, GROUP * C), F32),
            pltpu.VMEM((C, GROUP * C), BF),
            pltpu.VMEM((21 * C, PAIR), BF),
            pltpu.VMEM((20 * C, PAIR), BF),
            pltpu.VMEM((20 * C, PAIR), BF),
            pltpu.VMEM((19 * C, PAIR), BF),
            pltpu.VMEM((36 * C, C), F32),
            pltpu.VMEM((38 * C, C), BF),
            pltpu.VMEM((EXT // GROUP * C, C), BF),
            pltpu.VMEM((ROWS, C, C), BF),
            pltpu.SemaphoreType.DMA(()),
        ]
        + [pltpu.VMEM((4 * C, 3 * PAIR), BF)] * 4,
        compiler_params=params(32),
        name="middle_layers",
        cost_estimate=pl.CostEstimate(flops=12 * 10**9, bytes_accessed=16 * MIB, transcendentals=10**6),
    )(
        *messages,
        col_map,
        lift_weight,
        conv_bias,
        hidden,
        slope0,
        ocean,
        sensitivity,
        low,
        high,
        conv_weight,
    )
    projects = [project] + [lax.ppermute(project, "tile", by_mate(2 * s)) for s in range(1, SENT)]
    own_projects = jnp.concatenate(projects, axis=0)
    mate_projects = lax.ppermute(own_projects, "tile", by_mate(1))

    sums = pl.pallas_call(
        functools.partial(scatter_kernel, planes),
        out_shape=tuple(shape(F * ROWS, C) for _ in range(planes)),
        scratch_shapes=[
            pltpu.VMEM((GROUP * ROWS, F * C), BF),
            pltpu.VMEM((planes * F * ROWS, C), F32),
        ],
        compiler_params=params(8),
        name="scatter",
    )(scatter, own_projects, mate_projects)
    act0, *sums = lax.optimization_barrier((act0, *sums))
    sums = [sums[0]] + [lax.ppermute(sums[z], "tile", by_plane(-z)) for z in range(1, planes)]
    state_grad = pl.pallas_call(
        last_kernel,
        out_shape=shape(ROWS, C, C),
        scratch_shapes=[pltpu.VMEM((17 * C, PAIR), BF), pltpu.VMEM((4 * C, 3 * PAIR), BF)],
        compiler_params=params(14),
        name="last_adjoint",
        cost_estimate=pl.CostEstimate(flops=3 * 10**9, bytes_accessed=6 * MIB, transcendentals=0),
    )(act0, grad1, conv_weight)

    panel_grad = sum(block.astype(F32) for block in sums)
    panels = forcing.shape[0]
    panel_grad = panel_grad.reshape(panels, F, 8, C).transpose(0, 2, 1, 3)
    return imitated, state_grad, panel_grad


def solution(mesh):
    in_specs = (
        P(("member", "tile"), None, None, None),
        P(("member", "tile"), None, None),
        P(("member", "tile"), None, None),
        P("tile", None),
        P("tile", None),
        P("tile", None),
        P("tile", None),
        P(),
        P("tile", None),
        P(),
        P(),
        P(),
    )
    out_specs = (
        P(("member", "tile"), None, None),
        P(("member", "tile"), None, None),
        P(("member", "tile"), None, None, None),
    )
    return jax.shard_map(body, mesh=mesh, in_specs=in_specs, out_specs=out_specs, check_vma=False)
```

```python
import functools

import jax
import jax.numpy as jnp
from jax import lax
from jax.experimental import pallas as pl
from jax.experimental.pallas import tpu as pltpu
from jax.sharding import PartitionSpec as P

F = 10
FP = 16
K = 4
C = 128
ROWS = 32
EXT = 48
PAD = 8
GROUP = 8
SENT = GROUP // 2
STEP = 1
PAIR = 2 * C
BF = jnp.bfloat16
F32 = jnp.float32
MIB = 1 << 20


def params(mib):
    return pltpu.CompilerParams(vmem_limit_bytes=mib * MIB)


def dot(a, b, dims=(((1,), (0,)), ((), ()))):
    return lax.dot_general(a, b, dims, preferred_element_type=F32)


def split(x):
    high = x.astype(BF)
    return high, (x - high.astype(F32)).astype(BF)


def fine_dot(a, b, dims=(((1,), (0,)), ((), ()))):
    ah, al = split(a)
    bh, bl = split(b)
    return dot(ah, bh, dims) + (dot(ah, bl, dims) + dot(al, bh, dims))


def pair_rows(index, count=1):
    start = index * C
    if not isinstance(index, int):
        start = pl.multiple_of(start, C)
    return pl.ds(start, count * C)


def store_pair(xp, index, value):
    xp[pair_rows(index), :] = value.astype(BF)


def centre(xp, index):
    low = xp[pair_rows(index), C:]
    high = xp[pair_rows(index + 1), :C]
    return jnp.concatenate([low, high], axis=1).astype(F32)


def two_rows(ref, row):
    start = row * C
    if not isinstance(row, int):
        start = pl.multiple_of(start, C)
    low = ref[pl.ds(start, C), :]
    high = ref[pl.ds(start + C, C), :]
    return jnp.concatenate([low, high], axis=1).astype(F32)


def layer(xp, taps, count, step, finish):
    sub_row = lax.broadcasted_iota(jnp.int32, (8, PAIR), 0)
    for first in range(0, count, step):
        size = min(step, count - first)
        seen = jnp.concatenate(
            [xp[pair_rows(first, size), :], xp[pair_rows(first + 1, size), :]], axis=1
        )
        parts = [dot(seen, taps[:, b * PAIR : (b + 1) * PAIR]) for b in range(3)]
        for j in range(size):
            rows = slice(j * C, (j + 1) * C)
            before = pltpu.roll(parts[0][rows], 1, 0)
            before = jnp.concatenate([jnp.where(sub_row == 0, 0.0, before[:8]), before[8:]], axis=0)
            after = pltpu.roll(parts[2][rows], C - 1, 0)
            after = jnp.concatenate([after[:-8], jnp.where(sub_row == 7, 0.0, after[-8:])], axis=0)
            finish(first + j, parts[1][rows] + before + after)


def by_field(value, field):
    panels = value.shape[0] // (F * 8)
    part = value.reshape(panels, F, 8, C)[:, field]
    return part.reshape(panels * 8, C)


def column_tables(table, devices):
    entries = [table[jnp.clip(device, 0, table.shape[0] - 1)] for device in devices]
    fill = jnp.zeros((C - 2 * K * len(entries), C), F32)
    return jnp.concatenate(entries + [fill], axis=0).T


def picked(columns, place, ident, start, size):
    total = jnp.zeros((size, ident.shape[1]), F32)
    part = columns[start : start + size]
    for k in range(K):
        at = place * 2 * K + k
        total += jnp.where(part[:, at : at + 1] == ident, part[:, at + K : at + K + 1], 0.0)
    return total


def source_ident(planes, plane, spot, sides):
    lane = lax.broadcasted_iota(jnp.int32, (1, sides * planes * ROWS), 1)
    from_plane = lax.rem(plane - (lane // ROWS) % planes + planes, planes)
    from_spot = jnp.where(lane < planes * ROWS, spot, spot ^ 1)
    return ((from_plane * GROUP + from_spot) * ROWS + lane % ROWS).astype(F32)


def pick_kernel(planes, table, picks):
    me = lax.axis_index("tile")
    plane, spot = me // GROUP, me % GROUP
    count = planes * GROUP
    ident = source_ident(planes, plane, spot, 2)
    devices = [plane * GROUP + (spot ^ s) + step for s in range(0, GROUP, 2) for step in (-1, 0, 1)]
    columns = column_tables(table, devices)
    parts = []
    for place, device in enumerate(devices):
        start, size = ((ROWS - PAD, PAD), (0, ROWS), (0, PAD))[place % 3]
        inside = jnp.logical_and(device >= 0, device < count)
        parts.append(jnp.where(inside, picked(columns, place, ident, start, size), 0.0))
    picks[...] = jnp.concatenate(parts, axis=0).astype(BF)


def matrix_kernel(planes, table, scatter):
    me = lax.axis_index("tile")
    plane, spot = me // GROUP, me % GROUP
    ident = source_ident(planes, plane, spot, 1)
    columns = column_tables(table, [plane * GROUP + (spot ^ s) for s in range(GROUP)])
    parts = [picked(columns, s, ident, 0, ROWS) for s in range(GROUP)]
    scatter[...] = jnp.concatenate(parts, axis=0).T.astype(BF)


def message_kernel(planes, picks, own, mate, *refs):
    outs, wide = refs[:-1], refs[-1]
    sources = planes * ROWS
    for side, block in enumerate((own, mate)):
        value = block[...].astype(F32)
        for f in range(F):
            wide[side * sources : (side + 1) * sources, f * C : (f + 1) * C] = by_field(
                value, f
            ).astype(BF)
    for f in range(F):
        found = dot(picks[...], wide[:, f * C : (f + 1) * C]).astype(BF)
        for n, out in enumerate(outs):
            out[f * EXT : (f + 1) * EXT, :] = found[n * EXT : (n + 1) * EXT]


def fill_taps(taps, weight, l, back):
    zero = jnp.zeros((C, C), BF)
    for b in range(3):
        taps[0:C, b * PAIR + C : (b + 1) * PAIR] = zero
        taps[3 * C :, b * PAIR : b * PAIR + C] = zero
        for a in range(3):
            if back:
                block = weight[l, 2 - a, 2 - b].astype(F32).T.astype(BF)
            else:
                block = weight[l, a, b]
            for half in range(2):
                start = b * PAIR + half * C
                taps[(a + half) * C : (a + half + 1) * C, start : start + C] = block


def edge_rows(pair, other, start, size):
    odd = lax.rem(lax.axis_index("tile"), 2) == 1
    mine, next_one = pair[start : start + size, :].astype(F32), other[start : start + size, :].astype(F32)
    return jnp.where(odd, mine, next_one), jnp.where(odd, next_one, mine)


def first_kernel(ice, pair, other, mask, weight, bias, hidden, slope, ocean, xp, taps):
    fill_taps(taps, weight, 0, False)

    def ice_row(r):
        if r < 0:
            return edge_rows(pair, other, (r + 6) * C, C)[0]
        if r >= ROWS:
            return edge_rows(pair, other, (r - ROWS) * C, C)[1]
        return ice[r].astype(F32)

    for p in range(22):
        row = 2 * p - 6
        store_pair(xp, p, jnp.concatenate([ice_row(row), ice_row(row + 1)], axis=1))
    before, after = edge_rows(pair, other, 9 * C, 2 * PAD)
    cells = jnp.concatenate([before[:PAD], mask[...].astype(F32), after[:PAD]], axis=0)
    cells = jnp.concatenate([cells, jnp.zeros((C - EXT, C), F32)], axis=0).T
    for r in range(-5, 37):
        column = jnp.broadcast_to(cells[:, r + PAD : r + PAD + 1], (C, C))
        ocean[(r + 5) * C : (r + 6) * C, :] = column.astype(BF)
    both = jnp.concatenate([bias[0:1, :], bias[0:1, :]], axis=1)

    def finish(p, total):
        tangent = jnp.tanh(total + both)
        cell = two_rows(ocean, 2 * p)
        moved = cell * tangent
        slope[pair_rows(p), :] = (cell - moved * tangent).astype(BF)
        hidden[pair_rows(p), :] = (centre(xp, p) + moved).astype(BF)

    layer(xp, taps, 21, STEP, finish)


def main_kernel(*refs):
    messages = refs[:SENT]
    (col_map, lift, bias, hidden, slope0, ocean, sens, pair, other, weight) = refs[SENT : SENT + 10]
    imitated, act0, grad1, project = refs[SENT + 10 : SENT + 14]
    ice, lifted, diag, xa, xb, slope1, slope2, grads, out_rows, turned, shown, sem, *taps = refs[SENT + 14 :]
    w1f, w2f, w2b, w1b = taps
    for n, (l, back) in enumerate(((1, False), (2, False), (2, True), (1, True))):
        fill_taps(taps[n], weight, l, back)
    ice[...] = jnp.zeros(ice.shape, F32)
    for f in range(F):
        rows = slice(f * EXT, (f + 1) * EXT)
        total = messages[0][rows, :].astype(F32)
        for s in range(1, SENT):
            total += messages[s][rows, :].astype(F32)
        ice[:, f, :] = fine_dot(total, col_map[...])
    diag[...] = jnp.zeros(diag.shape, BF)
    for j in range(GROUP):
        diag[j * FP : j * FP + F, j * C : (j + 1) * C] = lift[...]
    for group in range(EXT // GROUP):
        block = ice[group * GROUP : (group + 1) * GROUP].reshape(C, C)
        turned[group * C : (group + 1) * C, :] = block.T.astype(BF)
    for group in range(EXT // GROUP):
        lifted[group * C : (group + 1) * C, :] = dot(
            turned[group * C : (group + 1) * C, :], diag[...]
        )

    def lifted_row(r):
        e = r + PAD
        return lifted[(e // 8) * C : (e // 8 + 1) * C, (e % 8) * C : (e % 8 + 1) * C]

    for p in range(21):
        row = 2 * p - 5
        add = jnp.concatenate([lifted_row(row), lifted_row(row + 1)], axis=1)
        store_pair(xa, p, hidden[pair_rows(p), :].astype(F32) + add)

    def bias_of(l):
        return jnp.concatenate([bias[l : l + 1, :], bias[l : l + 1, :]], axis=1)

    bias1, bias2 = bias_of(1), bias_of(2)

    def finish1(p, total):
        tangent = jnp.tanh(total + bias1)
        cell = two_rows(ocean, 2 * p + 1)
        moved = cell * tangent
        slope1[pair_rows(p), :] = (cell - moved * tangent).astype(BF)
        store_pair(xb, p, centre(xa, p) + moved)

    layer(xa, w1f, 20, STEP, finish1)

    def finish2(p, total):
        tangent = jnp.tanh(total + bias2)
        cell = two_rows(ocean, 2 * p + 2)
        moved = cell * tangent
        slope2[pair_rows(p), :] = (cell - moved * tangent).astype(BF)
        value = (centre(xb, p) + moved).astype(BF)
        for half in range(2):
            row = 2 * p + half - 3
            if 0 <= row < ROWS:
                shown[row] = value[:, half * C : half * C + C]

    layer(xb, w2f, 19, STEP, finish2)
    copy = pltpu.make_async_copy(shown, imitated, sem)
    copy.start()

    def sens_row(r):
        if r < 0:
            return edge_rows(pair, other, (r + 9) * C, C)[0]
        if r >= ROWS:
            return edge_rows(pair, other, (r - ROWS + 6) * C, C)[1]
        return sens[r].astype(F32)

    for p in range(19):
        row = 2 * p - 3
        value = jnp.concatenate([sens_row(row), sens_row(row + 1)], axis=1)
        store_pair(xa, p, value * slope2[pair_rows(p), :].astype(F32))
        out_rows[pair_rows(2 * p), :] = value[:, :C].astype(BF)
        out_rows[pair_rows(2 * p + 1), :] = value[:, C:].astype(BF)

    def finish3(p, total):
        total += two_rows(out_rows, 2 * p + 1)
        grads[pair_rows(2 * p), :] = total[:, :C]
        grads[pair_rows(2 * p + 1), :] = total[:, C:]
        store_pair(xb, p, total * slope1[pair_rows(p + 1), :].astype(F32))

    layer(xa, w2b, 18, STEP, finish3)

    def finish4(p, total):
        total += two_rows(grads, 2 * p + 1)
        act0[pair_rows(p), :] = (total * slope0[pair_rows(p + 2), :].astype(F32)).astype(BF)
        grad1[pair_rows(2 * p), :] = total[:, :C]
        grad1[pair_rows(2 * p + 1), :] = total[:, C:]

    layer(xb, w1b, 17, STEP, finish4)
    short = jnp.concatenate([lift[...].astype(F32), jnp.zeros((FP - F, C), F32)], axis=0).astype(BF)
    nt = (((1,), (1,)), ((), ()))
    for r in range(ROWS):
        part = dot(short, grad1[(r + 1) * C : (r + 2) * C, :].astype(BF), nt)
        ice[r, :, :] = part
    ice[0:ROWS] = fine_dot(ice[0:ROWS].reshape(ROWS * FP, C), col_map[...], nt).reshape(ROWS, FP, C)
    for f in range(F):
        project[f * ROWS : (f + 1) * ROWS, :] = ice[0:ROWS, f, :].astype(BF)
    copy.wait()


def last_kernel(act0, grad1, weight, out, xp, taps):
    fill_taps(taps, weight, 0, True)
    for p in range(17):
        store_pair(xp, p, act0[pair_rows(p), :].astype(F32))

    def finish(p, total):
        total += two_rows(grad1, 2 * p + 1)
        out[2 * p] = total[:, :C].astype(BF)
        out[2 * p + 1] = total[:, C:].astype(BF)

    layer(xp, taps, 16, STEP, finish)


def scatter_kernel(planes, scatter, own, mate, *refs):
    outs, wide, found = refs[:-2], refs[-2], refs[-1]
    for s in range(GROUP):
        block, row = (own, mate)[s % 2], (s // 2) * F * ROWS
        for f in range(F):
            wide[s * ROWS : (s + 1) * ROWS, f * C : (f + 1) * C] = block[
                row + f * ROWS : row + (f + 1) * ROWS, :
            ]
    for f in range(F):
        part = dot(scatter[...], wide[:, f * C : (f + 1) * C])
        for panel in range(planes * ROWS // 8):
            row = (panel * F + f) * 8
            found[row : row + 8, :] = part[panel * 8 : panel * 8 + 8]
    for z in range(planes):
        outs[z][...] = found[z * F * ROWS : (z + 1) * F * ROWS, :].astype(BF)


def shape(*dims, dtype=BF):
    return jax.ShapeDtypeStruct(dims, dtype)


def body(
    forcing,
    ice_state,
    sensitivity,
    owner_device,
    panel_slot,
    row_offset,
    intersection_weight,
    col_map,
    ocean_mask,
    lift_weight,
    conv_weight,
    conv_bias,
):
    count = lax.axis_size("tile")
    planes = count // GROUP

    def by_plane(step):
        return [(i, (i + GROUP * step) % count) for i in range(count)]

    def by_mate(step):
        return [(i, i ^ step) for i in range(count)]

    def spread(array, above):
        array = jnp.pad(array.T, ((K * above, K - K * above), (0, C - ROWS)))
        return jnp.broadcast_to(array[None], (count, 2 * K, C))

    ident = (spread(owner_device, 0) * 4 + spread(panel_slot, 0)) * 8 + spread(row_offset, 0)
    table = ident.astype(F32) + spread(intersection_weight, 1)
    ready = table
    table = lax.all_to_all(table, "tile", 0, 0, tiled=True)
    fields = forcing.transpose(0, 2, 1, 3).reshape(F * ROWS, C)
    blocks = [fields] + [lax.ppermute(fields, "tile", by_plane(z)) for z in range(1, planes)]
    own_column = jnp.concatenate(blocks, axis=0)
    mate_column = lax.ppermute(own_column, "tile", by_mate(1))

    rows_sent = 9 * C + 2 * PAD

    def window(array, start, size, place):
        array = lax.slice_in_dim(array, start, start + size)
        return jnp.pad(array, ((place, rows_sent - place - size), (0, 0)))

    def edge(arrays, ice_row, sens_row, mask_row):
        ice, sens, mask = arrays
        return (
            window(ice.reshape(ROWS * C, C), ice_row * C, 6 * C, 0)
            + window(sens.reshape(ROWS * C, C), sens_row * C, 3 * C, 6 * C)
            + jnp.where(window(mask, mask_row, PAD, 9 * C) == 1, 1.0, 0.0).astype(BF)
        )

    arrays = (ice_state, sensitivity, ocean_mask)
    to_next = edge(arrays, ROWS - 6, ROWS - 3, ROWS - PAD)
    to_last = edge(lax.optimization_barrier(arrays), 0, 0, 0)
    picks = pl.pallas_call(
        functools.partial(pick_kernel, planes),
        out_shape=shape(SENT * EXT, 2 * planes * ROWS),
        compiler_params=params(4),
        name="picks",
        cost_estimate=pl.CostEstimate(flops=10**10, bytes_accessed=MIB, transcendentals=0),
    )(table)
    messages = pl.pallas_call(
        functools.partial(message_kernel, planes),
        out_shape=tuple(shape(F * EXT, C) for _ in range(SENT)),
        scratch_shapes=[pltpu.VMEM((2 * planes * ROWS, F * C), BF)],
        compiler_params=params(10),
        name="messages",
    )(picks, own_column, mate_column)
    odd = lax.rem(lax.axis_index("tile"), 2) == 1
    to_pair, to_other = jnp.where(odd, to_last, to_next), jnp.where(odd, to_next, to_last)
    to_pair, to_other, _ = lax.optimization_barrier((to_pair, to_other, ready))
    pair = lax.ppermute(to_pair, "tile", by_mate(1))
    across = [(i, i + 1) for i in range(1, count - 1, 2)]
    other = lax.ppermute(to_other, "tile", across + [(b, a) for a, b in across])
    messages = [messages[0]] + [
        lax.ppermute(messages[s], "tile", by_mate(2 * s)) for s in range(1, SENT)
    ]
    hidden, slope0, ocean = pl.pallas_call(
        first_kernel,
        out_shape=(shape(21 * C, PAIR), shape(21 * C, PAIR), shape(42 * C, C)),
        scratch_shapes=[pltpu.VMEM((22 * C, PAIR), BF), pltpu.VMEM((4 * C, 3 * PAIR), BF)],
        compiler_params=params(14),
        name="first_layer",
        cost_estimate=pl.CostEstimate(flops=4 * 10**9, bytes_accessed=8 * MIB, transcendentals=10**6),
    )(ice_state, pair, other, ocean_mask, conv_weight, conv_bias)

    imitated, act0, grad1, project = pl.pallas_call(
        main_kernel,
        out_shape=(
            shape(ROWS, C, C),
            shape(17 * C, PAIR),
            shape(34 * C, C, dtype=F32),
            shape(F * ROWS, C),
        ),
        out_specs=(pl.BlockSpec(memory_space=pltpu.HBM),)
        + (pl.BlockSpec(memory_space=pltpu.VMEM),) * 3,
        scratch_shapes=[
            pltpu.VMEM((EXT, FP, C), F32),
            pltpu.VMEM((EXT // GROUP * C, GROUP * C), F32),
            pltpu.VMEM((C, GROUP * C), BF),
            pltpu.VMEM((21 * C, PAIR), BF),
            pltpu.VMEM((20 * C, PAIR), BF),
            pltpu.VMEM((20 * C, PAIR), BF),
            pltpu.VMEM((19 * C, PAIR), BF),
            pltpu.VMEM((36 * C, C), F32),
            pltpu.VMEM((38 * C, C), BF),
            pltpu.VMEM((EXT // GROUP * C, C), BF),
            pltpu.VMEM((ROWS, C, C), BF),
            pltpu.SemaphoreType.DMA(()),
        ]
        + [pltpu.VMEM((4 * C, 3 * PAIR), BF)] * 4,
        compiler_params=params(32),
        name="middle_layers",
        cost_estimate=pl.CostEstimate(flops=12 * 10**9, bytes_accessed=16 * MIB, transcendentals=10**6),
    )(
        *messages,
        col_map,
        lift_weight,
        conv_bias,
        hidden,
        slope0,
        ocean,
        sensitivity,
        pair,
        other,
        conv_weight,
    )
    table, project = lax.optimization_barrier((table, project))
    scatter = pl.pallas_call(
        functools.partial(matrix_kernel, planes),
        out_shape=shape(planes * ROWS, GROUP * ROWS),
        compiler_params=params(4),
        name="matrix",
        cost_estimate=pl.CostEstimate(flops=10**9, bytes_accessed=MIB, transcendentals=0),
    )(table)
    projects = [project] + [lax.ppermute(project, "tile", by_mate(2 * s)) for s in range(1, SENT)]
    own_projects = jnp.concatenate(projects, axis=0)
    mate_projects = lax.ppermute(own_projects, "tile", by_mate(1))

    sums = pl.pallas_call(
        functools.partial(scatter_kernel, planes),
        out_shape=tuple(shape(F * ROWS, C) for _ in range(planes)),
        scratch_shapes=[
            pltpu.VMEM((GROUP * ROWS, F * C), BF),
            pltpu.VMEM((planes * F * ROWS, C), F32),
        ],
        compiler_params=params(8),
        name="scatter",
    )(scatter, own_projects, mate_projects)
    act0, *sums = lax.optimization_barrier((act0, *sums))
    sums = [sums[0]] + [lax.ppermute(sums[z], "tile", by_plane(-z)) for z in range(1, planes)]
    state_grad = pl.pallas_call(
        last_kernel,
        out_shape=shape(ROWS, C, C),
        scratch_shapes=[pltpu.VMEM((17 * C, PAIR), BF), pltpu.VMEM((4 * C, 3 * PAIR), BF)],
        compiler_params=params(14),
        name="last_adjoint",
        cost_estimate=pl.CostEstimate(flops=3 * 10**9, bytes_accessed=6 * MIB, transcendentals=0),
    )(act0, grad1, conv_weight)

    panel_grad = sum(block.astype(F32) for block in sums)
    panels = forcing.shape[0]
    panel_grad = panel_grad.reshape(panels, F, 8, C).transpose(0, 2, 1, 3)
    return imitated, state_grad, panel_grad


def solution(mesh):
    in_specs = (
        P(("member", "tile"), None, None, None),
        P(("member", "tile"), None, None),
        P(("member", "tile"), None, None),
        P("tile", None),
        P("tile", None),
        P("tile", None),
        P("tile", None),
        P(),
        P("tile", None),
        P(),
        P(),
        P(),
    )
    out_specs = (
        P(("member", "tile"), None, None),
        P(("member", "tile"), None, None),
        P(("member", "tile"), None, None, None),
    )
    return jax.shard_map(body, mesh=mesh, in_specs=in_specs, out_specs=out_specs, check_vma=False)
```

```python
import functools

import jax
import jax.numpy as jnp
from jax import lax
from jax.experimental import pallas as pl
from jax.experimental.pallas import tpu as pltpu
from jax.sharding import PartitionSpec as P

F = 10
FP = 16
K = 4
C = 128
ROWS = 32
EXT = 48
PAD = 8
GROUP = 8
SENT = GROUP // 2
STEP = 1
PAIR = 2 * C
BF = jnp.bfloat16
F32 = jnp.float32
MIB = 1 << 20


def params(mib):
    return pltpu.CompilerParams(vmem_limit_bytes=mib * MIB)


def dot(a, b, dims=(((1,), (0,)), ((), ()))):
    return lax.dot_general(a, b, dims, preferred_element_type=F32)


def split(x):
    high = x.astype(BF)
    return high, (x - high.astype(F32)).astype(BF)


def fine_dot(a, b, dims=(((1,), (0,)), ((), ()))):
    ah, al = split(a)
    bh, bl = split(b)
    return dot(ah, bh, dims) + (dot(ah, bl, dims) + dot(al, bh, dims))


def pair_rows(index, count=1):
    start = index * C
    if not isinstance(index, int):
        start = pl.multiple_of(start, C)
    return pl.ds(start, count * C)


def store_pair(xp, index, value):
    xp[pair_rows(index), :] = value.astype(BF)


def centre(xp, index):
    low = xp[pair_rows(index), C:]
    high = xp[pair_rows(index + 1), :C]
    return jnp.concatenate([low, high], axis=1).astype(F32)


def two_rows(ref, row):
    start = row * C
    if not isinstance(row, int):
        start = pl.multiple_of(start, C)
    low = ref[pl.ds(start, C), :]
    high = ref[pl.ds(start + C, C), :]
    return jnp.concatenate([low, high], axis=1).astype(F32)


def layer(xp, taps, count, step, finish):
    sub_row = lax.broadcasted_iota(jnp.int32, (8, PAIR), 0)
    for first in range(0, count, step):
        size = min(step, count - first)
        seen = jnp.concatenate(
            [xp[pair_rows(first, size), :], xp[pair_rows(first + 1, size), :]], axis=1
        )
        parts = [dot(seen, taps[:, b * PAIR : (b + 1) * PAIR]) for b in range(3)]
        for j in range(size):
            rows = slice(j * C, (j + 1) * C)
            before = pltpu.roll(parts[0][rows], 1, 0)
            before = jnp.concatenate([jnp.where(sub_row == 0, 0.0, before[:8]), before[8:]], axis=0)
            after = pltpu.roll(parts[2][rows], C - 1, 0)
            after = jnp.concatenate([after[:-8], jnp.where(sub_row == 7, 0.0, after[-8:])], axis=0)
            finish(first + j, parts[1][rows] + before + after)


def by_field(value, field):
    panels = value.shape[0] // (F * 8)
    part = value.reshape(panels, F, 8, C)[:, field]
    return part.reshape(panels * 8, C)


def column_tables(table, devices):
    entries = [table[jnp.clip(device, 0, table.shape[0] - 1)] for device in devices]
    fill = jnp.zeros((C - 2 * K * len(entries), C), F32)
    return jnp.concatenate(entries + [fill], axis=0).T


def picked(columns, place, ident, start, size):
    total = jnp.zeros((size, ident.shape[1]), F32)
    part = columns[start : start + size]
    for k in range(K):
        at = place * 2 * K + k
        total += jnp.where(part[:, at : at + 1] == ident, part[:, at + K : at + K + 1], 0.0)
    return total


def source_ident(planes, plane, spot, sides):
    lane = lax.broadcasted_iota(jnp.int32, (1, sides * planes * ROWS), 1)
    from_plane = lax.rem(plane - (lane // ROWS) % planes + planes, planes)
    from_spot = jnp.where(lane < planes * ROWS, spot, spot ^ 1)
    return ((from_plane * GROUP + from_spot) * ROWS + lane % ROWS).astype(F32)


def pick_kernel(planes, table, picks, scatter):
    me = lax.axis_index("tile")
    plane, spot = me // GROUP, me % GROUP
    count = planes * GROUP
    ident = source_ident(planes, plane, spot, 2)
    devices = [plane * GROUP + (spot ^ s) + step for s in range(0, GROUP, 2) for step in (-1, 0, 1)]
    columns = column_tables(table, devices)
    parts = []
    for place, device in enumerate(devices):
        start, size = ((ROWS - PAD, PAD), (0, ROWS), (0, PAD))[place % 3]
        inside = jnp.logical_and(device >= 0, device < count)
        parts.append(jnp.where(inside, picked(columns, place, ident, start, size), 0.0))
    picks[...] = jnp.concatenate(parts, axis=0).astype(BF)
    ident = source_ident(planes, plane, spot, 1)
    columns = column_tables(table, [plane * GROUP + (spot ^ s) for s in range(GROUP)])
    parts = [picked(columns, s, ident, 0, ROWS) for s in range(GROUP)]
    scatter[...] = jnp.concatenate(parts, axis=0).T.astype(BF)


def message_kernel(planes, picks, own, mate, *refs):
    outs, wide = refs[:-1], refs[-1]
    sources = planes * ROWS
    for side, block in enumerate((own, mate)):
        value = block[...].astype(F32)
        for f in range(F):
            wide[side * sources : (side + 1) * sources, f * C : (f + 1) * C] = by_field(
                value, f
            ).astype(BF)
    for f in range(F):
        found = dot(picks[...], wide[:, f * C : (f + 1) * C]).astype(BF)
        for n, out in enumerate(outs):
            out[f * EXT : (f + 1) * EXT, :] = found[n * EXT : (n + 1) * EXT]


def fill_taps(taps, weight, l, back):
    zero = jnp.zeros((C, C), BF)
    for b in range(3):
        taps[0:C, b * PAIR + C : (b + 1) * PAIR] = zero
        taps[3 * C :, b * PAIR : b * PAIR + C] = zero
        for a in range(3):
            if back:
                block = weight[l, 2 - a, 2 - b].astype(F32).T.astype(BF)
            else:
                block = weight[l, a, b]
            for half in range(2):
                start = b * PAIR + half * C
                taps[(a + half) * C : (a + half + 1) * C, start : start + C] = block


def edge_rows(pair, other, start, size):
    odd = lax.rem(lax.axis_index("tile"), 2) == 1
    mine, next_one = pair[start : start + size, :].astype(F32), other[start : start + size, :].astype(F32)
    return jnp.where(odd, mine, next_one), jnp.where(odd, next_one, mine)


def first_kernel(ice, pair, other, mask, weight, bias, hidden, slope, ocean, xp, taps):
    fill_taps(taps, weight, 0, False)

    def ice_row(r):
        if r < 0:
            return edge_rows(pair, other, (r + 6) * C, C)[0]
        if r >= ROWS:
            return edge_rows(pair, other, (r - ROWS) * C, C)[1]
        return ice[r].astype(F32)

    for p in range(22):
        row = 2 * p - 6
        store_pair(xp, p, jnp.concatenate([ice_row(row), ice_row(row + 1)], axis=1))
    before, after = edge_rows(pair, other, 9 * C, 2 * PAD)
    cells = jnp.concatenate([before[:PAD], mask[...].astype(F32), after[:PAD]], axis=0)
    cells = jnp.concatenate([cells, jnp.zeros((C - EXT, C), F32)], axis=0).T
    for r in range(-5, 37):
        column = jnp.broadcast_to(cells[:, r + PAD : r + PAD + 1], (C, C))
        ocean[(r + 5) * C : (r + 6) * C, :] = column.astype(BF)
    both = jnp.concatenate([bias[0:1, :], bias[0:1, :]], axis=1)

    def finish(p, total):
        tangent = jnp.tanh(total + both)
        cell = two_rows(ocean, 2 * p)
        moved = cell * tangent
        slope[pair_rows(p), :] = (cell - moved * tangent).astype(BF)
        hidden[pair_rows(p), :] = (centre(xp, p) + moved).astype(BF)

    layer(xp, taps, 21, STEP, finish)


def main_kernel(*refs):
    messages = refs[:SENT]
    (col_map, lift, bias, hidden, slope0, ocean, sens, pair, other, weight) = refs[SENT : SENT + 10]
    imitated, act0, grad1, project = refs[SENT + 10 : SENT + 14]
    ice, lifted, diag, xa, xb, slope1, slope2, grads, out_rows, turned, shown, sem, *taps = refs[SENT + 14 :]
    w1f, w2f, w2b, w1b = taps
    for n, (l, back) in enumerate(((1, False), (2, False), (2, True), (1, True))):
        fill_taps(taps[n], weight, l, back)
    ice[...] = jnp.zeros(ice.shape, F32)
    for f in range(F):
        rows = slice(f * EXT, (f + 1) * EXT)
        total = messages[0][rows, :].astype(F32)
        for s in range(1, SENT):
            total += messages[s][rows, :].astype(F32)
        ice[:, f, :] = fine_dot(total, col_map[...])
    diag[...] = jnp.zeros(diag.shape, BF)
    for j in range(GROUP):
        diag[j * FP : j * FP + F, j * C : (j + 1) * C] = lift[...]
    for group in range(EXT // GROUP):
        block = ice[group * GROUP : (group + 1) * GROUP].reshape(C, C)
        turned[group * C : (group + 1) * C, :] = block.T.astype(BF)
    for group in range(EXT // GROUP):
        lifted[group * C : (group + 1) * C, :] = dot(
            turned[group * C : (group + 1) * C, :], diag[...]
        )

    def lifted_row(r):
        e = r + PAD
        return lifted[(e // 8) * C : (e // 8 + 1) * C, (e % 8) * C : (e % 8 + 1) * C]

    for p in range(21):
        row = 2 * p - 5
        add = jnp.concatenate([lifted_row(row), lifted_row(row + 1)], axis=1)
        store_pair(xa, p, hidden[pair_rows(p), :].astype(F32) + add)

    def bias_of(l):
        return jnp.concatenate([bias[l : l + 1, :], bias[l : l + 1, :]], axis=1)

    bias1, bias2 = bias_of(1), bias_of(2)

    def finish1(p, total):
        tangent = jnp.tanh(total + bias1)
        cell = two_rows(ocean, 2 * p + 1)
        moved = cell * tangent
        slope1[pair_rows(p), :] = (cell - moved * tangent).astype(BF)
        store_pair(xb, p, centre(xa, p) + moved)

    layer(xa, w1f, 20, STEP, finish1)

    def finish2(p, total):
        tangent = jnp.tanh(total + bias2)
        cell = two_rows(ocean, 2 * p + 2)
        moved = cell * tangent
        slope2[pair_rows(p), :] = (cell - moved * tangent).astype(BF)
        value = (centre(xb, p) + moved).astype(BF)
        for half in range(2):
            row = 2 * p + half - 3
            if 0 <= row < ROWS:
                shown[row] = value[:, half * C : half * C + C]

    layer(xb, w2f, 19, STEP, finish2)
    copy = pltpu.make_async_copy(shown, imitated, sem)
    copy.start()

    def sens_row(r):
        if r < 0:
            return edge_rows(pair, other, (r + 9) * C, C)[0]
        if r >= ROWS:
            return edge_rows(pair, other, (r - ROWS + 6) * C, C)[1]
        return sens[r].astype(F32)

    for p in range(19):
        row = 2 * p - 3
        value = jnp.concatenate([sens_row(row), sens_row(row + 1)], axis=1)
        store_pair(xa, p, value * slope2[pair_rows(p), :].astype(F32))
        out_rows[pair_rows(2 * p), :] = value[:, :C].astype(BF)
        out_rows[pair_rows(2 * p + 1), :] = value[:, C:].astype(BF)

    def finish3(p, total):
        total += two_rows(out_rows, 2 * p + 1)
        grads[pair_rows(2 * p), :] = total[:, :C]
        grads[pair_rows(2 * p + 1), :] = total[:, C:]
        store_pair(xb, p, total * slope1[pair_rows(p + 1), :].astype(F32))

    layer(xa, w2b, 18, STEP, finish3)

    def finish4(p, total):
        total += two_rows(grads, 2 * p + 1)
        act0[pair_rows(p), :] = (total * slope0[pair_rows(p + 2), :].astype(F32)).astype(BF)
        grad1[pair_rows(2 * p), :] = total[:, :C]
        grad1[pair_rows(2 * p + 1), :] = total[:, C:]

    layer(xb, w1b, 17, STEP, finish4)
    short = jnp.concatenate([lift[...].astype(F32), jnp.zeros((FP - F, C), F32)], axis=0).astype(BF)
    nt = (((1,), (1,)), ((), ()))
    for r in range(ROWS):
        part = dot(short, grad1[(r + 1) * C : (r + 2) * C, :].astype(BF), nt)
        ice[r, :, :] = part
    ice[0:ROWS] = fine_dot(ice[0:ROWS].reshape(ROWS * FP, C), col_map[...], nt).reshape(ROWS, FP, C)
    for f in range(F):
        project[f * ROWS : (f + 1) * ROWS, :] = ice[0:ROWS, f, :].astype(BF)
    copy.wait()


def last_kernel(act0, grad1, weight, out, xp, taps):
    fill_taps(taps, weight, 0, True)
    for p in range(17):
        store_pair(xp, p, act0[pair_rows(p), :].astype(F32))

    def finish(p, total):
        total += two_rows(grad1, 2 * p + 1)
        out[2 * p] = total[:, :C].astype(BF)
        out[2 * p + 1] = total[:, C:].astype(BF)

    layer(xp, taps, 16, STEP, finish)


def scatter_kernel(planes, scatter, own, mate, *refs):
    outs, wide, found = refs[:-2], refs[-2], refs[-1]
    for s in range(GROUP):
        block, row = (own, mate)[s % 2], (s // 2) * F * ROWS
        for f in range(F):
            wide[s * ROWS : (s + 1) * ROWS, f * C : (f + 1) * C] = block[
                row + f * ROWS : row + (f + 1) * ROWS, :
            ]
    for f in range(F):
        part = dot(scatter[...], wide[:, f * C : (f + 1) * C])
        for panel in range(planes * ROWS // 8):
            row = (panel * F + f) * 8
            found[row : row + 8, :] = part[panel * 8 : panel * 8 + 8]
    for z in range(planes):
        outs[z][...] = found[z * F * ROWS : (z + 1) * F * ROWS, :].astype(BF)


def shape(*dims, dtype=BF):
    return jax.ShapeDtypeStruct(dims, dtype)


def body(
    forcing,
    ice_state,
    sensitivity,
    owner_device,
    panel_slot,
    row_offset,
    intersection_weight,
    col_map,
    ocean_mask,
    lift_weight,
    conv_weight,
    conv_bias,
):
    count = lax.axis_size("tile")
    planes = count // GROUP

    def by_plane(step):
        return [(i, (i + GROUP * step) % count) for i in range(count)]

    def by_mate(step):
        return [(i, i ^ step) for i in range(count)]

    def spread(array, above):
        array = jnp.pad(array.T, ((K * above, K - K * above), (0, C - ROWS)))
        return jnp.broadcast_to(array[None], (count, 2 * K, C))

    ident = (spread(owner_device, 0) * 4 + spread(panel_slot, 0)) * 8 + spread(row_offset, 0)
    table = ident.astype(F32) + spread(intersection_weight, 1)
    ready = table
    table = lax.all_to_all(table, "tile", 0, 0, tiled=True)
    fields = forcing.transpose(0, 2, 1, 3).reshape(F * ROWS, C)
    blocks = [fields] + [lax.ppermute(fields, "tile", by_plane(z)) for z in range(1, planes)]
    own_column = jnp.concatenate(blocks, axis=0)
    mate_column = lax.ppermute(own_column, "tile", by_mate(1))

    rows_sent = 9 * C + 2 * PAD

    def window(array, start, size, place):
        array = lax.slice_in_dim(array, start, start + size)
        return jnp.pad(array, ((place, rows_sent - place - size), (0, 0)))

    def edge(arrays, ice_row, sens_row, mask_row):
        ice, sens, mask = arrays
        return (
            window(ice.reshape(ROWS * C, C), ice_row * C, 6 * C, 0)
            + window(sens.reshape(ROWS * C, C), sens_row * C, 3 * C, 6 * C)
            + jnp.where(window(mask, mask_row, PAD, 9 * C) == 1, 1.0, 0.0).astype(BF)
        )

    arrays = (ice_state, sensitivity, ocean_mask)
    to_next = edge(arrays, ROWS - 6, ROWS - 3, ROWS - PAD)
    to_last = edge(lax.optimization_barrier(arrays), 0, 0, 0)
    picks, scatter = pl.pallas_call(
        functools.partial(pick_kernel, planes),
        out_shape=(shape(SENT * EXT, 2 * planes * ROWS), shape(planes * ROWS, GROUP * ROWS)),
        compiler_params=params(4),
        name="picks",
        cost_estimate=pl.CostEstimate(flops=10**10, bytes_accessed=MIB, transcendentals=0),
    )(table)
    messages = pl.pallas_call(
        functools.partial(message_kernel, planes),
        out_shape=tuple(shape(F * EXT, C) for _ in range(SENT)),
        scratch_shapes=[pltpu.VMEM((2 * planes * ROWS, F * C), BF)],
        compiler_params=params(10),
        name="messages",
    )(picks, own_column, mate_column)
    odd = lax.rem(lax.axis_index("tile"), 2) == 1
    to_pair, to_other = jnp.where(odd, to_last, to_next), jnp.where(odd, to_next, to_last)
    to_pair, to_other, _ = lax.optimization_barrier((to_pair, to_other, ready))
    pair = lax.ppermute(to_pair, "tile", by_mate(1))
    across = [(i, i + 1) for i in range(1, count - 1, 2)]
    other = lax.ppermute(to_other, "tile", across + [(b, a) for a, b in across])
    messages = [messages[0]] + [
        lax.ppermute(messages[s], "tile", by_mate(2 * s)) for s in range(1, SENT)
    ]
    hidden, slope0, ocean = pl.pallas_call(
        first_kernel,
        out_shape=(shape(21 * C, PAIR), shape(21 * C, PAIR), shape(42 * C, C)),
        scratch_shapes=[pltpu.VMEM((22 * C, PAIR), BF), pltpu.VMEM((4 * C, 3 * PAIR), BF)],
        compiler_params=params(14),
        name="first_layer",
        cost_estimate=pl.CostEstimate(flops=4 * 10**9, bytes_accessed=8 * MIB, transcendentals=10**6),
    )(ice_state, pair, other, ocean_mask, conv_weight, conv_bias)

    imitated, act0, grad1, project = pl.pallas_call(
        main_kernel,
        out_shape=(
            shape(ROWS, C, C),
            shape(17 * C, PAIR),
            shape(34 * C, C, dtype=F32),
            shape(F * ROWS, C),
        ),
        out_specs=(pl.BlockSpec(memory_space=pltpu.HBM),)
        + (pl.BlockSpec(memory_space=pltpu.VMEM),) * 3,
        scratch_shapes=[
            pltpu.VMEM((EXT, FP, C), F32),
            pltpu.VMEM((EXT // GROUP * C, GROUP * C), F32),
            pltpu.VMEM((C, GROUP * C), BF),
            pltpu.VMEM((21 * C, PAIR), BF),
            pltpu.VMEM((20 * C, PAIR), BF),
            pltpu.VMEM((20 * C, PAIR), BF),
            pltpu.VMEM((19 * C, PAIR), BF),
            pltpu.VMEM((36 * C, C), F32),
            pltpu.VMEM((38 * C, C), BF),
            pltpu.VMEM((EXT // GROUP * C, C), BF),
            pltpu.VMEM((ROWS, C, C), BF),
            pltpu.SemaphoreType.DMA(()),
        ]
        + [pltpu.VMEM((4 * C, 3 * PAIR), BF)] * 4,
        compiler_params=params(32),
        name="middle_layers",
        cost_estimate=pl.CostEstimate(flops=12 * 10**9, bytes_accessed=16 * MIB, transcendentals=10**6),
    )(
        *messages,
        col_map,
        lift_weight,
        conv_bias,
        hidden,
        slope0,
        ocean,
        sensitivity,
        pair,
        other,
        conv_weight,
    )
    projects = [project] + [lax.ppermute(project, "tile", by_mate(2 * s)) for s in range(1, SENT)]
    own_projects = jnp.concatenate(projects, axis=0)
    mate_projects = lax.ppermute(own_projects, "tile", by_mate(1))

    sums = pl.pallas_call(
        functools.partial(scatter_kernel, planes),
        out_shape=tuple(shape(F * ROWS, C) for _ in range(planes)),
        scratch_shapes=[
            pltpu.VMEM((GROUP * ROWS, F * C), BF),
            pltpu.VMEM((planes * F * ROWS, C), F32),
        ],
        compiler_params=params(8),
        name="scatter",
    )(scatter, own_projects, mate_projects)
    act0, *sums = lax.optimization_barrier((act0, *sums))
    sums = [sums[0]] + [lax.ppermute(sums[z], "tile", by_plane(-z)) for z in range(1, planes)]
    state_grad = pl.pallas_call(
        last_kernel,
        out_shape=shape(ROWS, C, C),
        scratch_shapes=[pltpu.VMEM((17 * C, PAIR), BF), pltpu.VMEM((4 * C, 3 * PAIR), BF)],
        compiler_params=params(14),
        name="last_adjoint",
        cost_estimate=pl.CostEstimate(flops=3 * 10**9, bytes_accessed=6 * MIB, transcendentals=0),
    )(act0, grad1, conv_weight)

    panel_grad = sum(block.astype(F32) for block in sums)
    panels = forcing.shape[0]
    panel_grad = panel_grad.reshape(panels, F, 8, C).transpose(0, 2, 1, 3)
    return imitated, state_grad, panel_grad


def solution(mesh):
    in_specs = (
        P(("member", "tile"), None, None, None),
        P(("member", "tile"), None, None),
        P(("member", "tile"), None, None),
        P("tile", None),
        P("tile", None),
        P("tile", None),
        P("tile", None),
        P(),
        P("tile", None),
        P(),
        P(),
        P(),
    )
    out_specs = (
        P(("member", "tile"), None, None),
        P(("member", "tile"), None, None),
        P(("member", "tile"), None, None, None),
    )
    return jax.shard_map(body, mesh=mesh, in_specs=in_specs, out_specs=out_specs, check_vma=False)
```

```python
import functools

import jax
import jax.numpy as jnp
from jax import lax
from jax.experimental import pallas as pl
from jax.experimental.pallas import tpu as pltpu
from jax.sharding import PartitionSpec as P

F = 10
FP = 16
K = 4
C = 128
ROWS = 32
EXT = 48
PAD = 8
SEEN = 42
SHIP = 432
GROUP = 8
SENT = GROUP // 2
STEP = 1
PAIR = 2 * C
BF = jnp.bfloat16
F32 = jnp.float32
MIB = 1 << 20


def params(mib):
    return pltpu.CompilerParams(vmem_limit_bytes=mib * MIB)


def dot(a, b, dims=(((1,), (0,)), ((), ()))):
    return lax.dot_general(a, b, dims, preferred_element_type=F32)


def split(x):
    high = x.astype(BF)
    return high, (x - high.astype(F32)).astype(BF)


def fine_dot(a, b, dims=(((1,), (0,)), ((), ()))):
    ah, al = split(a)
    bh, bl = split(b)
    return dot(ah, bh, dims) + (dot(ah, bl, dims) + dot(al, bh, dims))


def pair_rows(index, count=1):
    start = index * C
    if not isinstance(index, int):
        start = pl.multiple_of(start, C)
    return pl.ds(start, count * C)


def store_pair(xp, index, value):
    xp[pair_rows(index), :] = value.astype(BF)


def centre(xp, index):
    low = xp[pair_rows(index), C:]
    high = xp[pair_rows(index + 1), :C]
    return jnp.concatenate([low, high], axis=1).astype(F32)


def two_rows(ref, row):
    start = row * C
    if not isinstance(row, int):
        start = pl.multiple_of(start, C)
    low = ref[pl.ds(start, C), :]
    high = ref[pl.ds(start + C, C), :]
    return jnp.concatenate([low, high], axis=1).astype(F32)


def layer(xp, taps, count, step, finish):
    sub_row = lax.broadcasted_iota(jnp.int32, (8, PAIR), 0)
    for first in range(0, count, step):
        size = min(step, count - first)
        seen = jnp.concatenate(
            [xp[pair_rows(first, size), :], xp[pair_rows(first + 1, size), :]], axis=1
        )
        parts = [dot(seen, taps[:, b * PAIR : (b + 1) * PAIR]) for b in range(3)]
        for j in range(size):
            rows = slice(j * C, (j + 1) * C)
            before = pltpu.roll(parts[0][rows], 1, 0)
            before = jnp.concatenate([jnp.where(sub_row == 0, 0.0, before[:8]), before[8:]], axis=0)
            after = pltpu.roll(parts[2][rows], C - 1, 0)
            after = jnp.concatenate([after[:-8], jnp.where(sub_row == 7, 0.0, after[-8:])], axis=0)
            finish(first + j, parts[1][rows] + before + after)


def by_field(value, field):
    panels = value.shape[0] // (F * 8)
    part = value.reshape(panels, F, 8, C)[:, field]
    return part.reshape(panels * 8, C)


def column_tables(table, devices):
    entries = [table[jnp.clip(device, 0, table.shape[0] - 1)] for device in devices]
    fill = jnp.zeros((C - 2 * K * len(entries), C), F32)
    return jnp.concatenate(entries + [fill], axis=0).T


def picked(columns, place, ident, start, size):
    total = jnp.zeros((size, ident.shape[1]), F32)
    part = columns[start : start + size]
    for k in range(K):
        at = place * 2 * K + k
        total += jnp.where(part[:, at : at + 1] == ident, part[:, at + K : at + K + 1], 0.0)
    return total


def source_ident(planes, plane, spot, sides):
    lane = lax.broadcasted_iota(jnp.int32, (1, sides * planes * ROWS), 1)
    from_plane = lax.rem(plane - (lane // ROWS) % planes + planes, planes)
    from_spot = jnp.where(lane < planes * ROWS, spot, spot ^ 1)
    return ((from_plane * GROUP + from_spot) * ROWS + lane % ROWS).astype(F32)


def pick_kernel(planes, table, picks, scatter):
    me = lax.axis_index("tile")
    plane, spot = me // GROUP, me % GROUP
    count = planes * GROUP
    ident = source_ident(planes, plane, spot, 2)
    devices = [plane * GROUP + (spot ^ s) + step for s in range(0, GROUP, 2) for step in (-1, 0, 1)]
    columns = column_tables(table, devices)
    parts = []
    for place, device in enumerate(devices):
        start, size = ((ROWS - PAD, PAD), (0, ROWS), (0, PAD))[place % 3]
        inside = jnp.logical_and(device >= 0, device < count)
        parts.append(jnp.where(inside, picked(columns, place, ident, start, size), 0.0))
    picks[...] = jnp.concatenate(parts, axis=0).astype(BF)
    ident = source_ident(planes, plane, spot, 1)
    columns = column_tables(table, [plane * GROUP + (spot ^ s) for s in range(GROUP)])
    parts = [picked(columns, s, ident, 0, ROWS) for s in range(GROUP)]
    scatter[...] = jnp.concatenate(parts, axis=0).T.astype(BF)


def message_kernel(planes, picks, own, mate, *refs):
    outs, wide, packed = refs[:-2], refs[-2], refs[-1]
    sources = planes * ROWS
    for side, block in enumerate((own, mate)):
        value = block[...].astype(F32)
        for f in range(F):
            wide[side * sources : (side + 1) * sources, f * C : (f + 1) * C] = by_field(
                value, f
            ).astype(BF)
    for f in range(F):
        found = dot(picks[...], wide[:, f * C : (f + 1) * C])
        for n in range(SENT):
            packed[n, f * SEEN : (f + 1) * SEEN, :] = found[n * EXT + 3 : n * EXT + 3 + SEEN]
    for n, out in enumerate(outs):
        packed[n, F * SEEN :, :] = jnp.zeros((SHIP - F * SEEN, C), F32)
        out[...] = packed[n].astype(BF)


def fill_taps(taps, weight, l, back):
    zero = jnp.zeros((C, C), BF)
    for b in range(3):
        taps[0:C, b * PAIR + C : (b + 1) * PAIR] = zero
        taps[3 * C :, b * PAIR : b * PAIR + C] = zero
        for a in range(3):
            if back:
                block = weight[l, 2 - a, 2 - b].astype(F32).T.astype(BF)
            else:
                block = weight[l, a, b]
            for half in range(2):
                start = b * PAIR + half * C
                taps[(a + half) * C : (a + half + 1) * C, start : start + C] = block


def edge_rows(pair, other, start, size):
    odd = lax.rem(lax.axis_index("tile"), 2) == 1
    mine, next_one = pair[start : start + size, :].astype(F32), other[start : start + size, :].astype(F32)
    return jnp.where(odd, mine, next_one), jnp.where(odd, next_one, mine)


def first_kernel(ice, pair, other, mask, weight, bias, hidden, slope, ocean, xp, taps):
    fill_taps(taps, weight, 0, False)

    def ice_row(r):
        if r < 0:
            return edge_rows(pair, other, (r + 6) * C, C)[0]
        if r >= ROWS:
            return edge_rows(pair, other, (r - ROWS) * C, C)[1]
        return ice[r].astype(F32)

    for p in range(22):
        row = 2 * p - 6
        store_pair(xp, p, jnp.concatenate([ice_row(row), ice_row(row + 1)], axis=1))
    before, after = edge_rows(pair, other, 9 * C, 2 * PAD)
    cells = jnp.concatenate([before[:PAD], mask[...].astype(F32), after[:PAD]], axis=0)
    cells = jnp.concatenate([cells, jnp.zeros((C - EXT, C), F32)], axis=0).T
    for r in range(-5, 37):
        column = jnp.broadcast_to(cells[:, r + PAD : r + PAD + 1], (C, C))
        ocean[(r + 5) * C : (r + 6) * C, :] = column.astype(BF)
    both = jnp.concatenate([bias[0:1, :], bias[0:1, :]], axis=1)

    def finish(p, total):
        tangent = jnp.tanh(total + both)
        cell = two_rows(ocean, 2 * p)
        moved = cell * tangent
        slope[pair_rows(p), :] = (cell - moved * tangent).astype(BF)
        hidden[pair_rows(p), :] = (centre(xp, p) + moved).astype(BF)

    layer(xp, taps, 21, STEP, finish)


def main_kernel(*refs):
    messages = refs[:SENT]
    (col_map, lift, bias, hidden, slope0, ocean, sens, pair, other, weight) = refs[SENT : SENT + 10]
    imitated, act0, grad1, project = refs[SENT + 10 : SENT + 14]
    ice, lifted, diag, xa, xb, slope1, slope2, grads, out_rows, turned, shown, sem, *taps = refs[SENT + 14 :]
    w1f, w2f, w2b, w1b = taps
    for n, (l, back) in enumerate(((1, False), (2, False), (2, True), (1, True))):
        fill_taps(taps[n], weight, l, back)
    ice[...] = jnp.zeros(ice.shape, F32)
    total = messages[0][...].astype(F32)
    for s in range(1, SENT):
        total += messages[s][...].astype(F32)
    lifted[0:SHIP, 0:C] = total
    for f in range(F):
        ice[3 : 3 + SEEN, f, :] = fine_dot(lifted[f * SEEN : (f + 1) * SEEN, 0:C], col_map[...])
    diag[...] = jnp.zeros(diag.shape, BF)
    for j in range(GROUP):
        diag[j * FP : j * FP + F, j * C : (j + 1) * C] = lift[...]
    for group in range(EXT // GROUP):
        block = ice[group * GROUP : (group + 1) * GROUP].reshape(C, C)
        turned[group * C : (group + 1) * C, :] = block.T.astype(BF)
    for group in range(EXT // GROUP):
        lifted[group * C : (group + 1) * C, :] = dot(
            turned[group * C : (group + 1) * C, :], diag[...]
        )

    def lifted_row(r):
        e = r + PAD
        return lifted[(e // 8) * C : (e // 8 + 1) * C, (e % 8) * C : (e % 8 + 1) * C]

    for p in range(21):
        row = 2 * p - 5
        add = jnp.concatenate([lifted_row(row), lifted_row(row + 1)], axis=1)
        store_pair(xa, p, hidden[pair_rows(p), :].astype(F32) + add)

    def bias_of(l):
        return jnp.concatenate([bias[l : l + 1, :], bias[l : l + 1, :]], axis=1)

    bias1, bias2 = bias_of(1), bias_of(2)

    def finish1(p, total):
        tangent = jnp.tanh(total + bias1)
        cell = two_rows(ocean, 2 * p + 1)
        moved = cell * tangent
        slope1[pair_rows(p), :] = (cell - moved * tangent).astype(BF)
        store_pair(xb, p, centre(xa, p) + moved)

    layer(xa, w1f, 20, STEP, finish1)

    def finish2(p, total):
        tangent = jnp.tanh(total + bias2)
        cell = two_rows(ocean, 2 * p + 2)
        moved = cell * tangent
        slope2[pair_rows(p), :] = (cell - moved * tangent).astype(BF)
        value = (centre(xb, p) + moved).astype(BF)
        for half in range(2):
            row = 2 * p + half - 3
            if 0 <= row < ROWS:
                shown[row] = value[:, half * C : half * C + C]

    layer(xb, w2f, 19, STEP, finish2)
    copy = pltpu.make_async_copy(shown, imitated, sem)
    copy.start()

    def sens_row(r):
        if r < 0:
            return edge_rows(pair, other, (r + 9) * C, C)[0]
        if r >= ROWS:
            return edge_rows(pair, other, (r - ROWS + 6) * C, C)[1]
        return sens[r].astype(F32)

    for p in range(19):
        row = 2 * p - 3
        value = jnp.concatenate([sens_row(row), sens_row(row + 1)], axis=1)
        store_pair(xa, p, value * slope2[pair_rows(p), :].astype(F32))
        out_rows[pair_rows(2 * p), :] = value[:, :C].astype(BF)
        out_rows[pair_rows(2 * p + 1), :] = value[:, C:].astype(BF)

    def finish3(p, total):
        total += two_rows(out_rows, 2 * p + 1)
        grads[pair_rows(2 * p), :] = total[:, :C]
        grads[pair_rows(2 * p + 1), :] = total[:, C:]
        store_pair(xb, p, total * slope1[pair_rows(p + 1), :].astype(F32))

    layer(xa, w2b, 18, STEP, finish3)

    def finish4(p, total):
        total += two_rows(grads, 2 * p + 1)
        act0[pair_rows(p), :] = (total * slope0[pair_rows(p + 2), :].astype(F32)).astype(BF)
        grad1[pair_rows(2 * p), :] = total[:, :C]
        grad1[pair_rows(2 * p + 1), :] = total[:, C:]

    layer(xb, w1b, 17, STEP, finish4)
    short = jnp.concatenate([lift[...].astype(F32), jnp.zeros((FP - F, C), F32)], axis=0).astype(BF)
    nt = (((1,), (1,)), ((), ()))
    for r in range(ROWS):
        part = dot(short, grad1[(r + 1) * C : (r + 2) * C, :].astype(BF), nt)
        ice[r, :, :] = part
    ice[0:ROWS] = fine_dot(ice[0:ROWS].reshape(ROWS * FP, C), col_map[...], nt).reshape(ROWS, FP, C)
    for f in range(F):
        project[f * ROWS : (f + 1) * ROWS, :] = ice[0:ROWS, f, :].astype(BF)
    copy.wait()


def last_kernel(act0, grad1, weight, out, xp, taps):
    fill_taps(taps, weight, 0, True)
    for p in range(17):
        store_pair(xp, p, act0[pair_rows(p), :].astype(F32))

    def finish(p, total):
        total += two_rows(grad1, 2 * p + 1)
        out[2 * p] = total[:, :C].astype(BF)
        out[2 * p + 1] = total[:, C:].astype(BF)

    layer(xp, taps, 16, STEP, finish)


def scatter_kernel(planes, scatter, own, mate, *refs):
    outs, wide, found = refs[:-2], refs[-2], refs[-1]
    for s in range(GROUP):
        block, row = (own, mate)[s % 2], (s // 2) * F * ROWS
        for f in range(F):
            wide[s * ROWS : (s + 1) * ROWS, f * C : (f + 1) * C] = block[
                row + f * ROWS : row + (f + 1) * ROWS, :
            ]
    for f in range(F):
        part = dot(scatter[...], wide[:, f * C : (f + 1) * C])
        for panel in range(planes * ROWS // 8):
            row = (panel * F + f) * 8
            found[row : row + 8, :] = part[panel * 8 : panel * 8 + 8]
    for z in range(planes):
        outs[z][...] = found[z * F * ROWS : (z + 1) * F * ROWS, :].astype(BF)


def shape(*dims, dtype=BF):
    return jax.ShapeDtypeStruct(dims, dtype)


def body(
    forcing,
    ice_state,
    sensitivity,
    owner_device,
    panel_slot,
    row_offset,
    intersection_weight,
    col_map,
    ocean_mask,
    lift_weight,
    conv_weight,
    conv_bias,
):
    count = lax.axis_size("tile")
    planes = count // GROUP

    def by_plane(step):
        return [(i, (i + GROUP * step) % count) for i in range(count)]

    def by_mate(step):
        return [(i, i ^ step) for i in range(count)]

    def spread(array, above):
        array = jnp.pad(array.T, ((K * above, K - K * above), (0, C - ROWS)))
        return jnp.broadcast_to(array[None], (count, 2 * K, C))

    ident = (spread(owner_device, 0) * 4 + spread(panel_slot, 0)) * 8 + spread(row_offset, 0)
    table = ident.astype(F32) + spread(intersection_weight, 1)
    ready = table
    table = lax.all_to_all(table, "tile", 0, 0, tiled=True)
    fields = forcing.transpose(0, 2, 1, 3).reshape(F * ROWS, C)
    blocks = [fields] + [lax.ppermute(fields, "tile", by_plane(z)) for z in range(1, planes)]
    own_column = jnp.concatenate(blocks, axis=0)
    mate_column = lax.ppermute(own_column, "tile", by_mate(1))

    rows_sent = 9 * C + 2 * PAD

    def window(array, start, size, place):
        array = lax.slice_in_dim(array, start, start + size)
        return jnp.pad(array, ((place, rows_sent - place - size), (0, 0)))

    def edge(arrays, ice_row, sens_row, mask_row):
        ice, sens, mask = arrays
        return (
            window(ice.reshape(ROWS * C, C), ice_row * C, 6 * C, 0)
            + window(sens.reshape(ROWS * C, C), sens_row * C, 3 * C, 6 * C)
            + jnp.where(window(mask, mask_row, PAD, 9 * C) == 1, 1.0, 0.0).astype(BF)
        )

    arrays = (ice_state, sensitivity, ocean_mask)
    to_next = edge(arrays, ROWS - 6, ROWS - 3, ROWS - PAD)
    to_last = edge(lax.optimization_barrier(arrays), 0, 0, 0)
    picks, scatter = pl.pallas_call(
        functools.partial(pick_kernel, planes),
        out_shape=(shape(SENT * EXT, 2 * planes * ROWS), shape(planes * ROWS, GROUP * ROWS)),
        compiler_params=params(4),
        name="picks",
        cost_estimate=pl.CostEstimate(flops=10**10, bytes_accessed=MIB, transcendentals=0),
    )(table)
    messages = pl.pallas_call(
        functools.partial(message_kernel, planes),
        out_shape=tuple(shape(SHIP, C) for _ in range(SENT)),
        scratch_shapes=[pltpu.VMEM((2 * planes * ROWS, F * C), BF), pltpu.VMEM((SENT, SHIP, C), F32)],
        compiler_params=params(10),
        name="messages",
    )(picks, own_column, mate_column)
    odd = lax.rem(lax.axis_index("tile"), 2) == 1
    to_pair, to_other = jnp.where(odd, to_last, to_next), jnp.where(odd, to_next, to_last)
    to_pair, to_other, _ = lax.optimization_barrier((to_pair, to_other, ready))
    pair = lax.ppermute(to_pair, "tile", by_mate(1))
    across = [(i, i + 1) for i in range(1, count - 1, 2)]
    other = lax.ppermute(to_other, "tile", across + [(b, a) for a, b in across])
    messages = [messages[0]] + [
        lax.ppermute(messages[s], "tile", by_mate(2 * s)) for s in range(1, SENT)
    ]
    hidden, slope0, ocean = pl.pallas_call(
        first_kernel,
        out_shape=(shape(21 * C, PAIR), shape(21 * C, PAIR), shape(42 * C, C)),
        scratch_shapes=[pltpu.VMEM((22 * C, PAIR), BF), pltpu.VMEM((4 * C, 3 * PAIR), BF)],
        compiler_params=params(14),
        name="first_layer",
        cost_estimate=pl.CostEstimate(flops=4 * 10**9, bytes_accessed=8 * MIB, transcendentals=10**6),
    )(ice_state, pair, other, ocean_mask, conv_weight, conv_bias)

    imitated, act0, grad1, project = pl.pallas_call(
        main_kernel,
        out_shape=(
            shape(ROWS, C, C),
            shape(17 * C, PAIR),
            shape(34 * C, C, dtype=F32),
            shape(F * ROWS, C),
        ),
        out_specs=(pl.BlockSpec(memory_space=pltpu.HBM),)
        + (pl.BlockSpec(memory_space=pltpu.VMEM),) * 3,
        scratch_shapes=[
            pltpu.VMEM((EXT, FP, C), F32),
            pltpu.VMEM((EXT // GROUP * C, GROUP * C), F32),
            pltpu.VMEM((C, GROUP * C), BF),
            pltpu.VMEM((21 * C, PAIR), BF),
            pltpu.VMEM((20 * C, PAIR), BF),
            pltpu.VMEM((20 * C, PAIR), BF),
            pltpu.VMEM((19 * C, PAIR), BF),
            pltpu.VMEM((36 * C, C), F32),
            pltpu.VMEM((38 * C, C), BF),
            pltpu.VMEM((EXT // GROUP * C, C), BF),
            pltpu.VMEM((ROWS, C, C), BF),
            pltpu.SemaphoreType.DMA(()),
        ]
        + [pltpu.VMEM((4 * C, 3 * PAIR), BF)] * 4,
        compiler_params=params(32),
        name="middle_layers",
        cost_estimate=pl.CostEstimate(flops=12 * 10**9, bytes_accessed=16 * MIB, transcendentals=10**6),
    )(
        *messages,
        col_map,
        lift_weight,
        conv_bias,
        hidden,
        slope0,
        ocean,
        sensitivity,
        pair,
        other,
        conv_weight,
    )
    projects = [project] + [lax.ppermute(project, "tile", by_mate(2 * s)) for s in range(1, SENT)]
    own_projects = jnp.concatenate(projects, axis=0)
    mate_projects = lax.ppermute(own_projects, "tile", by_mate(1))

    sums = pl.pallas_call(
        functools.partial(scatter_kernel, planes),
        out_shape=tuple(shape(F * ROWS, C) for _ in range(planes)),
        scratch_shapes=[
            pltpu.VMEM((GROUP * ROWS, F * C), BF),
            pltpu.VMEM((planes * F * ROWS, C), F32),
        ],
        compiler_params=params(8),
        name="scatter",
    )(scatter, own_projects, mate_projects)
    act0, *sums = lax.optimization_barrier((act0, *sums))
    sums = [sums[0]] + [lax.ppermute(sums[z], "tile", by_plane(-z)) for z in range(1, planes)]
    state_grad = pl.pallas_call(
        last_kernel,
        out_shape=shape(ROWS, C, C),
        scratch_shapes=[pltpu.VMEM((17 * C, PAIR), BF), pltpu.VMEM((4 * C, 3 * PAIR), BF)],
        compiler_params=params(14),
        name="last_adjoint",
        cost_estimate=pl.CostEstimate(flops=3 * 10**9, bytes_accessed=6 * MIB, transcendentals=0),
    )(act0, grad1, conv_weight)

    panel_grad = sum(block.astype(F32) for block in sums)
    panels = forcing.shape[0]
    panel_grad = panel_grad.reshape(panels, F, 8, C).transpose(0, 2, 1, 3)
    return imitated, state_grad, panel_grad


def solution(mesh):
    in_specs = (
        P(("member", "tile"), None, None, None),
        P(("member", "tile"), None, None),
        P(("member", "tile"), None, None),
        P("tile", None),
        P("tile", None),
        P("tile", None),
        P("tile", None),
        P(),
        P("tile", None),
        P(),
        P(),
        P(),
    )
    out_specs = (
        P(("member", "tile"), None, None),
        P(("member", "tile"), None, None),
        P(("member", "tile"), None, None, None),
    )
    return jax.shard_map(body, mesh=mesh, in_specs=in_specs, out_specs=out_specs, check_vma=False)
```
